32 devices in a mesh: replica: 8 (over y, x, core), shard: 4 (over z).
Axes of the slice: x: 2, y: 2, z: 4, core: 2. Of those that a mesh axis runs over, the one named last changes fastest.
Arguments:
- tokens_in: bfloat16 [16384, 1088], P(('replica', 'shard')), may hold values from -6 to 6
- lengths: int32 [32, 4], P(('replica', 'shard')), may hold values from 1 to 384, 512 in all within a row
- ln1_gain: bfloat16 [2, 1088], P(None, 'shard'), may hold values from 0.5 to 1.5
- ln1_bias: bfloat16 [2, 1088], P(None, 'shard'), may hold values from -1 to 1
- qkv_weight: bfloat16 [2, 1088, 3264], P(None, 'shard'), may hold values from -0.1875 to 0.1875
- query_bias: bfloat16 [2, 1088], P(None, 'shard'), may hold values from -1 to 1
- value_bias: bfloat16 [2, 1088], P(None, 'shard'), may hold values from -1 to 1
- out_weight: bfloat16 [2, 1088, 1088], P(None, 'shard'), may hold values from -0.75 to 0.75
- out_bias: bfloat16 [2, 1088], P(None, 'shard'), may hold values from -1 to 1
- ln2_gain: bfloat16 [2, 1088], P(None, 'shard'), may hold values from 0.5 to 1.5
- ln2_bias: bfloat16 [2, 1088], P(None, 'shard'), may hold values from -1 to 1
- up_weight: bfloat16 [2, 1088, 4352], P(None, 'shard'), may hold values from -0.1875 to 0.1875
- up_bias: bfloat16 [2, 4352], P(None, 'shard'), may hold values from -1 to 1
- down_weight: bfloat16 [2, 4352, 1088], P(None, 'shard'), may hold values from -0.09375 to 0.09375
- down_bias: bfloat16 [2, 1088], P(None, 'shard'), may hold values from -1 to 1
- cotangent: bfloat16 [16384, 1088], P(('replica', 'shard')), may hold values from -6 to 6
Outputs:
- block_out: bfloat16 [16384, 1088], P(('replica', 'shard'))
- grad_in: float32 [16384, 1088], P(('replica', 'shard'))
- grad_ln1_gain: float32 [2, 1088], P(None, 'shard')
- grad_ln1_bias: float32 [2, 1088], P(None, 'shard')
- grad_qkv_weight: float32 [2, 1088, 3264], P(None, 'shard')
- grad_query_bias: float32 [2, 1088], P(None, 'shard')
- grad_value_bias: float32 [2, 1088], P(None, 'shard')
- grad_out_weight: float32 [2, 1088, 1088], P(None, 'shard')
- grad_out_bias: float32 [2, 1088], P(None, 'shard')
- grad_ln2_gain: float32 [2, 1088], P(None, 'shard')
- grad_ln2_bias: float32 [2, 1088], P(None, 'shard')
- grad_up_weight: float32 [2, 1088, 4352], P(None, 'shard')
- grad_up_bias: float32 [2, 4352], P(None, 'shard')
- grad_down_weight: float32 [2, 4352, 1088], P(None, 'shard')
- grad_down_bias: float32 [2, 1088], P(None, 'shard')
The draws below stay inside these ranges and needn't reach their ends.
Inputs may be any that keep to these rules, and one draw needn't show every extreme that they name: Each device's row of 4 lengths sums to 512, and one of them equals 384.
All inputs are finite; a program needn't handle non-finite values.
Results may differ from the reference program's by a relative error of at most 0.02.
Values may be sent and summed in bfloat16 or wider, within the bound.
No kernel may reach another device: no remote copies, remote signals or barrier semaphores. Data moves between devices by JAX's collectives and lax.ppermute only.
A program may use at most 320 MiB of HBM per device.

```python
import math
import jax
import jax.numpy as jnp
import numpy as np
from jax import lax

D = 1088
HEADS = 17
HEAD = 64
FF = 4352
LAYERS = 2
TOK_DEV = 512
SEQ_DEV = 4
SEQ_MAX = 384
TOKENS = 16384
N_REPLICA = 8
N_SHARD = 4


def levels(key, dims, cuts, least, high):
    level = 1.0
    for dim, parts in cuts:
        heights = jax.random.uniform(jax.random.fold_in(jax.random.fold_in(key, 6), dim), (parts,), jnp.float32, least / len(cuts), high / len(cuts))
        level = level * jnp.repeat(jnp.exp(heights), dims[dim] // parts).reshape((-1,) + (1,) * (len(dims) - 1 - dim))
    return level


def split_up(count, total, reach, lean):
    portions = [(1 << 20) // math.isqrt(rank ** lean) + 1 for rank in range(2, count + 1)]
    rest, holding = total - reach - (count - 1), [1] * (count - 1)
    while rest > 0:
        candidates = [i for i in range(count - 1) if holding[i] < reach]
        mass, left = sum([portions[i] for i in candidates]), rest
        for i in candidates:
            addition = min(reach - holding[i], max(1, left * portions[i] // mass), rest)
            holding[i] = holding[i] + addition
            rest = rest - addition
    return np.array([reach] + holding)


def uneven_parts(stream_key, count, total, bound, skew):
    if count == 2:
        one = jax.random.randint(stream_key, (), max(1, total - bound), min(bound, total - 1) + 1)
        return jnp.stack([one, total - one])
    sizes = jnp.asarray(split_up(count, total, bound, skew), jnp.int32)
    pairs = (count - 1) // 2
    giver, sink = sizes[1:1 + 2 * pairs:2], sizes[2:2 + 2 * pairs:2]
    room = jnp.minimum(giver - 1, bound - sink)
    shifted = jax.random.randint(jax.random.fold_in(stream_key, 1), (pairs,), 0, 1 << 20) % (room + 1)
    sizes = sizes.at[1:1 + 2 * pairs:2].set(giver - shifted).at[2:2 + 2 * pairs:2].set(sink + shifted)
    return sizes[jax.random.permutation(jax.random.fold_in(stream_key, 2), count)]


def centred(own_key, shape, deviation, bound, pieces=(), kind=jnp.bfloat16):
    values = jax.random.normal(own_key, shape, jnp.float32) * deviation
    if len(pieces) > 0:
        values = levels(own_key, shape, pieces, -0.22, 0.18) * values
    return jnp.clip(values, min=-bound, max=bound).astype(kind)


def setup_inputs(seed: int = 0) -> dict:
    key_of = jax.random.split(jax.random.key(seed), 17)
    return {
        "tokens_in": centred(key_of[0], (TOKENS, D), 1.0, 6.0, ((0, 32),)),
        "lengths": jax.vmap(lambda own: uneven_parts(own, SEQ_DEV, TOK_DEV, SEQ_MAX, 2))(jax.random.split(key_of[1], (N_REPLICA * N_SHARD))).reshape((N_REPLICA * N_SHARD, SEQ_DEV)).astype(jnp.int32),
        "ln1_gain": jnp.clip(1.0 + 0.1 * jax.random.normal(key_of[2], (LAYERS, D), jnp.float32), 0.5, 1.5).astype(jnp.bfloat16),
        "ln1_bias": centred(key_of[3], (LAYERS, D), 0.2, 1.0, ((1, 4),)),
        "qkv_weight": centred(key_of[4], (LAYERS, D, 3 * D), D ** -0.5, 0.1875, ((1, 4),)),
        "query_bias": centred(key_of[5], (LAYERS, D), 0.2, 1.0, ((1, 4),)),
        "value_bias": centred(key_of[6], (LAYERS, D), 0.2, 1.0, ((1, 4),)),
        "out_weight": centred(key_of[7], (LAYERS, D, D), (D // 16) ** -0.5, 0.75, ((1, 4),)),
        "out_bias": centred(key_of[8], (LAYERS, D), 0.2, 1.0, ((1, 4),)),
        "ln2_gain": jnp.clip(1.0 + 0.1 * jax.random.normal(key_of[9], (LAYERS, D), jnp.float32), 0.5, 1.5).astype(jnp.bfloat16),
        "ln2_bias": centred(key_of[10], (LAYERS, D), 0.2, 1.0, ((1, 4),)),
        "up_weight": centred(key_of[11], (LAYERS, D, FF), D ** -0.5, 0.1875, ((1, 4),)),
        "up_bias": centred(key_of[12], (LAYERS, FF), 0.2, 1.0, ((1, 4),)),
        "down_weight": centred(key_of[13], (LAYERS, FF, D), FF ** -0.5, 0.09375, ((1, 4),)),
        "down_bias": centred(key_of[14], (LAYERS, D), 0.2, 1.0, ((1, 4),)),
        "cotangent": centred(key_of[15], (TOKENS, D), 1.0, 6.0, ((0, 32),)),
    }


norm_eps = 1e-05
score_scale = 0.125
masked_fill = -1e+30

@jax.custom_vjp
def low(v):
    return lax.optimization_barrier(v.astype(jnp.bfloat16)).astype(jnp.float32)

@jax.custom_vjp
def low_back(v):
    return v

def low_keep(v):
    return (low(v), None)

def low_pass(kept, grad):
    return (grad,)

def back_keep(v):
    return (v, None)

def back_low(kept, grad):
    return (low(grad),)
low.defvjp(low_keep, low_pass)
low_back.defvjp(back_keep, back_low)

def layer_norm(values, norm_gain, norm_shift):
    center = values - lax.optimization_barrier(jnp.mean(values, axis=-1, keepdims=True))
    spread = lax.optimization_barrier(jnp.mean(center * center, axis=-1, keepdims=True))
    return center * lax.rsqrt(spread + norm_eps) * norm_gain + norm_shift

def matmul(left, right):
    return jnp.dot(left, right, precision=lax.Precision.HIGHEST, preferred_element_type=jnp.float32)

def segment_ids(lengths):
    seq_ends = jnp.cumsum(lengths, axis=1).astype(jnp.int32)
    positions = jnp.arange(TOK_DEV, dtype=jnp.int32)
    return lax.optimization_barrier(jnp.sum((positions[None, :, None] >= seq_ends[:, None, :]).astype(jnp.int32), axis=2))

def attend_block(queries, key_rows, value_rows, segment):
    scores = low_back(jnp.einsum('qhd,khd->hqk', queries, key_rows, precision=lax.Precision.HIGHEST) * score_scale)
    positions = jnp.arange(TOK_DEV, dtype=jnp.int32)
    allowed = (segment[:, None] == segment[None, :]) & (positions[:, None] >= positions[None, :])
    scores = jnp.where(allowed[None], scores, masked_fill)
    row_max = lax.optimization_barrier(jnp.max(scores, axis=-1, keepdims=True))
    exponent = jnp.where(allowed[None], jnp.exp(scores - row_max), 0.0)
    attn_probs = low(exponent / lax.optimization_barrier(jnp.sum(exponent, axis=-1, keepdims=True)))
    return jnp.einsum('hqk,khd->qhd', attn_probs, value_rows, precision=lax.Precision.HIGHEST)

def residual_block(stream, weights, segment):
    norm1_gain, norm1_shift, qkv_weight, query_bias, value_bias, out_weight, out_bias, norm2_gain, norm2_shift, up_weight, up_bias, down_weight, down_bias = weights
    blocks = TOKENS // TOK_DEV
    normed = low(layer_norm(stream, norm1_gain, norm1_shift))
    qkv_bias = jnp.concatenate([query_bias, jnp.zeros_like(query_bias), value_bias])
    projected = low(low_back(matmul(normed, qkv_weight) + qkv_bias))

    def split_heads(portion):
        return portion.reshape(blocks, TOK_DEV, HEADS, HEAD)
    queries = split_heads(projected[:, :D])
    key_rows = split_heads(projected[:, D:2 * D])
    value_rows = split_heads(projected[:, 2 * D:])
    checked = jax.checkpoint(attend_block)
    mixed = lax.map(lambda member: checked(member[0], member[1], member[2], member[3]), (queries, key_rows, value_rows, segment))
    mixed = low(low_back(mixed.reshape(TOKENS, D)))
    after_attn = stream + low_back(matmul(mixed, out_weight) + out_bias)
    normed_two = low(layer_norm(after_attn, norm2_gain, norm2_shift))
    hidden_pre = low_back(matmul(normed_two, up_weight) + up_bias)
    activated = low(jax.nn.gelu(hidden_pre, approximate=True))
    return after_attn + low_back(matmul(activated, down_weight) + down_bias)

def reference(tokens_in, lengths, ln1_gain, ln1_bias, qkv_weight, query_bias, value_bias, out_weight, out_bias, ln2_gain, ln2_bias, up_weight, up_bias, down_weight, down_bias, cotangent):
    params = tuple((member.astype(jnp.float32) for member in (ln1_gain, ln1_bias, qkv_weight, query_bias, value_bias, out_weight, out_bias, ln2_gain, ln2_bias, up_weight, up_bias, down_weight, down_bias)))
    segment = segment_ids(lengths)

    def whole_stack(stream, weights):
        for layer_idx in range(LAYERS):
            stream = residual_block(stream, tuple((member[layer_idx] for member in weights)), segment)
        return stream
    result, pullback = jax.vjp(whole_stack, tokens_in.astype(jnp.float32), params)
    grad_stream, grad_params = pullback(cotangent.astype(jnp.float32))
    return (result.astype(jnp.bfloat16), grad_stream, grad_params[0], grad_params[1], grad_params[2], grad_params[3], grad_params[4], grad_params[5], grad_params[6], grad_params[7], grad_params[8], grad_params[9], grad_params[10], grad_params[11], grad_params[12])
```

```python
import functools

import jax
import jax.numpy as jnp
from jax import lax
from jax.experimental import pallas as pl
from jax.experimental.pallas import tpu as pltpu
from jax.sharding import PartitionSpec as P

HEADS = 17
HEAD = 64


norm_eps = 1e-05
score_scale = 0.125
masked_fill = -1e30


def layer_norm(values, norm_gain, norm_shift):
    center = values - jnp.mean(values, axis=-1, keepdims=True)
    spread = jnp.mean(center * center, axis=-1, keepdims=True)
    return center * lax.rsqrt(spread + norm_eps) * norm_gain + norm_shift


def gelu_tanh(values):
    return jax.nn.gelu(values, approximate=True)


def causal_mask(lengths, count):
    seq_ends = jnp.cumsum(lengths[0])
    positions = jnp.arange(count, dtype=jnp.int32)
    segment = jnp.sum((positions[:, None] >= seq_ends[None, :]).astype(jnp.int32), axis=1)
    return (segment[:, None] == segment[None, :]) & (positions[:, None] >= positions[None, :])


def split_heads(rows):
    return rows.reshape(rows.shape[0], HEADS, HEAD)


def three_parts(projected):
    width = projected.shape[1] // 3
    return (
        split_heads(projected[:, :width]),
        split_heads(projected[:, width : 2 * width]),
        split_heads(projected[:, 2 * width :]),
    )


def scores_of(queries, key_rows, allowed):
    scores = (
        jnp.einsum("qhd,khd->hqk", queries, key_rows, preferred_element_type=jnp.float32)
        * score_scale
    )
    return jnp.where(allowed[None], scores, masked_fill)


def attend(projected, allowed):
    queries, key_rows, value_rows = three_parts(projected)
    scores = scores_of(queries, key_rows, allowed)
    row_max = jnp.max(scores, axis=-1, keepdims=True)
    exponent = jnp.where(allowed[None], jnp.exp(scores - row_max), 0.0)
    totals = jnp.sum(exponent, axis=-1, keepdims=True)
    attn_probs = (exponent / totals).astype(jnp.bfloat16)
    mixed = jnp.einsum("hqk,khd->qhd", attn_probs, value_rows, preferred_element_type=jnp.float32)
    mixed = mixed.reshape(projected.shape[0], projected.shape[1] // 3)
    return (mixed.astype(jnp.bfloat16), row_max + jnp.log(totals))


def attend_back(projected, log_total, grad_mixed, allowed):
    count = projected.shape[0]
    width = projected.shape[1] // 3
    queries, key_rows, value_rows = three_parts(projected)
    grad_heads = split_heads(grad_mixed)
    scores = scores_of(queries, key_rows, allowed)
    attn_probs = jnp.where(allowed[None], jnp.exp(scores - log_total), 0.0)
    grad_values = jnp.einsum(
        "hqk,qhd->khd",
        attn_probs.astype(jnp.bfloat16),
        grad_heads,
        preferred_element_type=jnp.float32,
    )
    grad_probs = jnp.einsum(
        "qhd,khd->hqk", grad_heads, value_rows, preferred_element_type=jnp.float32
    )
    row_dot = jnp.sum(attn_probs * grad_probs, axis=-1, keepdims=True)
    grad_scores = (attn_probs * (grad_probs - row_dot)).astype(jnp.bfloat16)
    grad_queries = (
        jnp.einsum("hqk,khd->qhd", grad_scores, key_rows, preferred_element_type=jnp.float32)
        * score_scale
    )
    grad_keys = (
        jnp.einsum("hqk,qhd->khd", grad_scores, queries, preferred_element_type=jnp.float32)
        * score_scale
    )
    joined = jnp.concatenate(
        [
            grad_queries.reshape(count, width),
            grad_keys.reshape(count, width),
            grad_values.reshape(count, width),
        ],
        axis=1,
    )
    return joined.astype(jnp.bfloat16)


def dot_columns(rows, chunks):
    return jnp.concatenate(
        [jnp.dot(rows, chunk, preferred_element_type=jnp.float32) for chunk in chunks], axis=1
    )


def dot_columns_back(rows, chunks):
    width = chunks[0].shape[1]
    return sum(
        jnp.einsum(
            "te,de->td",
            rows[:, i * width : (i + 1) * width],
            chunk,
            preferred_element_type=jnp.float32,
        )
        for i, chunk in enumerate(chunks)
    )


def forward_layer(stream, weights, allowed):
    small, qkv_weight, out_weight, up_weight, down_weight = weights
    (
        norm1_gain,
        norm1_shift,
        query_bias,
        value_bias,
        out_bias,
        norm2_gain,
        norm2_shift,
        up_bias,
        down_bias,
    ) = small
    normed = layer_norm(
        stream, norm1_gain.astype(jnp.float32), norm1_shift.astype(jnp.float32)
    ).astype(jnp.bfloat16)
    qkv_bias = jnp.concatenate([query_bias, jnp.zeros_like(query_bias), value_bias]).astype(
        jnp.float32
    )
    projected = (dot_columns(normed, qkv_weight) + qkv_bias).astype(
        jnp.bfloat16
    )
    mixed, log_total = attend(projected, allowed)
    after_attn = (
        stream
        + dot_columns(mixed, out_weight)
        + out_bias.astype(jnp.float32)
    )
    normed_two = layer_norm(
        after_attn, norm2_gain.astype(jnp.float32), norm2_shift.astype(jnp.float32)
    ).astype(jnp.bfloat16)
    hidden_pre = dot_columns(normed_two, up_weight) + up_bias.astype(jnp.float32)
    activated = gelu_tanh(hidden_pre).astype(jnp.bfloat16)
    result = (
        after_attn
        + jnp.dot(activated, down_weight, preferred_element_type=jnp.float32)
        + down_bias.astype(jnp.float32)
    )
    return (
        result,
        (
            stream,
            normed,
            projected,
            mixed,
            log_total,
            after_attn,
            normed_two,
            hidden_pre,
            activated,
        ),
    )


def backward_layer(grad_out, weights, saved, allowed):
    small, qkv_weight, out_weight, up_weight, down_weight = weights
    (
        norm1_gain,
        norm1_shift,
        query_bias,
        value_bias,
        out_bias,
        norm2_gain,
        norm2_shift,
        up_bias,
        down_bias,
    ) = small
    stream, normed, projected, mixed, log_total, after_attn, normed_two, hidden_pre, activated = (
        saved
    )
    width = stream.shape[1]
    grad_branch = grad_out.astype(jnp.bfloat16)
    grad_down_bias = jnp.sum(grad_branch.astype(jnp.float32), axis=0)
    grad_act = jnp.einsum("td,fd->tf", grad_branch, down_weight, preferred_element_type=jnp.float32)
    gelu_value, gelu_pull = jax.vjp(gelu_tanh, hidden_pre)
    grad_pre = gelu_pull(grad_act)[0].astype(jnp.bfloat16)
    grad_up_bias = jnp.sum(grad_pre.astype(jnp.float32), axis=0)
    grad_normed_two = dot_columns_back(grad_pre, up_weight)
    norm_value, norm_pull = jax.vjp(
        layer_norm, after_attn, norm2_gain.astype(jnp.float32), norm2_shift.astype(jnp.float32)
    )
    grad_after, grad_gain_two, grad_shift_two = norm_pull(grad_normed_two)
    grad_after = grad_out + grad_after
    grad_attn = grad_after.astype(jnp.bfloat16)
    grad_out_bias = jnp.sum(grad_attn.astype(jnp.float32), axis=0)
    grad_mixed = dot_columns_back(grad_attn, out_weight).astype(jnp.bfloat16)
    grad_projected = attend_back(projected, log_total, grad_mixed, allowed)
    grad_query_bias = jnp.sum(grad_projected[:, :width].astype(jnp.float32), axis=0)
    grad_value_bias = jnp.sum(grad_projected[:, 2 * width :].astype(jnp.float32), axis=0)
    grad_normed = dot_columns_back(grad_projected, qkv_weight)
    first_value, first_pull = jax.vjp(
        layer_norm, stream, norm1_gain.astype(jnp.float32), norm1_shift.astype(jnp.float32)
    )
    grad_stream, grad_gain_one, grad_shift_one = first_pull(grad_normed)
    vectors = (
        grad_gain_one,
        grad_shift_one,
        grad_query_bias,
        grad_value_bias,
        grad_out_bias,
        grad_gain_two,
        grad_shift_two,
        grad_up_bias,
        grad_down_bias,
    )
    operands = (
        normed,
        grad_projected,
        mixed,
        grad_attn,
        normed_two,
        grad_pre,
        activated,
        grad_branch,
    )
    return (grad_after + grad_stream, vectors, operands)


class Layout:
    def __init__(self, mesh):
        self.copies = mesh.shape["replica"]
        self.shards = mesh.shape["shard"]
        self.across = self.copies // 4
        self.chips = self.copies // 2
        self.crossed = self.across == 2

    def index(self, a, b, c):
        return (a % self.across) * 4 + (b % 2) * 2 + c

    def pairs(self, way):
        out = []
        for i in range(self.copies):
            a, b, c = i // 4, (i // 2) % 2, i % 2
            turned = self.crossed and c == 1
            if way == "core":
                to = self.index(a, b, 1 - c)
            elif (way == "first") != turned:
                to = self.index(a, b + 1, c)
            else:
                to = self.index(a + 1, b, c)
            out.append((i, to))
        return out

    def move(self, value, way):
        return lax.ppermute(value, "replica", self.pairs(way))

    def place(self):
        r = lax.axis_index("replica")
        return r // 4, (r // 2) % 2, r % 2, lax.axis_index("shard")

    def chip_at(self, core, f, k):
        a, b, _, _ = self.place()
        plain = ((a + k) % self.across) * 2 + (b + f) % 2
        if not self.crossed:
            return plain
        turned = ((a + f) % self.across) * 2 + (b + k) % 2
        return jnp.where(core == 1, turned, plain)

    def slots(self):
        return [(f, k) for k in range(self.across) for f in range(2)]


def place_kernel(by_shard, index_ref, *refs):
    chips_cores = (len(refs) - 2)
    blocks, out_ref, sems = refs[:chips_cores], refs[chips_cores], refs[chips_cores + 1]
    shards = blocks[0].shape[0]
    copies = []
    for p in range(chips_cores):
        chip, core = index_ref[0, p], index_ref[1, p]
        for s in range(shards):
            shard = index_ref[2, s]
            target = out_ref.at[shard, chip, core] if by_shard else out_ref.at[chip, shard, core]
            copies.append(pltpu.make_async_copy(blocks[p].at[s], target, sems.at[p * shards + s]))
            copies[-1].start()
    for copy in copies:
        copy.wait()


def assemble(layout, blocks, by_shard):
    _, _, core, shard = layout.place()
    chips, shards = layout.chips, layout.shards
    own = [layout.chip_at(core, -f, -k) for f, k in layout.slots()]
    other = [layout.chip_at(1 - core, -f, -k) for f, k in layout.slots()]
    count = 2 * chips
    width = max(count, shards)

    def row(values):
        return jnp.stack(list(values) + [jnp.int32(0)] * (width - len(values)))

    index = jnp.stack(
        [
            row(own + other),
            row([core] * chips + [1 - core] * chips),
            row([(shard + s) % shards for s in range(shards)]),
        ]
    ).astype(jnp.int32)
    _, rows, cols = blocks[0].shape
    outer = (shards, chips) if by_shard else (chips, shards)
    return pl.pallas_call(
        functools.partial(place_kernel, by_shard),
        out_shape=jax.ShapeDtypeStruct(outer + (2, rows, cols), blocks[0].dtype),
        in_specs=[pl.BlockSpec(memory_space=pltpu.SMEM)]
        + [pl.BlockSpec(memory_space=pl.ANY)] * count,
        out_specs=pl.BlockSpec(memory_space=pltpu.VMEM),
        scratch_shapes=[pltpu.SemaphoreType.DMA((count * shards,))],
        compiler_params=pltpu.CompilerParams(vmem_limit_bytes=40 << 20),
        cost_estimate=pl.CostEstimate(
            flops=0, bytes_accessed=4 * count * shards * rows * cols, transcendentals=0
        ),
    )(index, *blocks)


def gather_shards(layout, piece):
    n = layout.shards
    _, _, _, shard = layout.place()
    right, left = [piece], [piece]
    for t in range(1, n):
        right.append(lax.ppermute(right[-1], "shard", [(i, i + 1) for i in range(t - 1, n - 1)]))
        left.append(lax.ppermute(left[-1], "shard", [(i, i - 1) for i in range(1, n - t + 1)]))
    parts = [piece] + [jnp.where(shard + k < n, left[k], right[n - k]) for k in range(1, n)]
    return jnp.stack(parts)


def gather_group(layout, piece, by_shard):
    block = gather_shards(layout, piece)
    held = {(0, 0): block}
    held[1, 0] = layout.move(block, "first")
    for k in range(1, layout.across):
        for f in range(2):
            held[f, k] = layout.move(held[f, k - 1], "second")
    own = [held[slot] for slot in layout.slots()]
    other = [layout.move(block, "core") for block in own]
    return assemble(layout, own + other, by_shard)


def add_low(left, right):
    return (left.astype(jnp.float32) + right.astype(jnp.float32)).astype(jnp.bfloat16)


def reduce_shards(layout, parts):
    n = layout.shards
    right = left = None
    for t in range(1, n):
        right = parts[n - t] if right is None else add_low(parts[n - t], right)
        left = parts[t] if left is None else add_low(parts[t], left)
        right = lax.ppermute(right, "shard", [(i, i + 1) for i in range(min(t, n - 1))])
        left = lax.ppermute(left, "shard", [(i, i - 1) for i in range(max(1, n - t), n)])
    total = parts[0].astype(jnp.float32) + right.astype(jnp.float32) + left.astype(jnp.float32)
    return total.astype(jnp.bfloat16)


def reduce_group(layout, product):
    _, _, core, _ = layout.place()
    n = layout.shards
    sums = {}
    for f, k in layout.slots():
        away = product(layout.chip_at(1 - core, f, k), 1 - core).astype(jnp.bfloat16)
        came = layout.move(away, "core")
        here = product(layout.chip_at(core, f, k), core)
        sums[f, k] = (here + came.astype(jnp.float32)).astype(jnp.bfloat16)
    halves = []
    for f in range(2):
        total = sums[f, layout.across - 1]
        for step in range(1, layout.across):
            total = add_low(layout.move(total, "second"), sums[f, layout.across - 1 - step])
        halves.append(total)
    total = add_low(layout.move(halves[1], "first"), halves[0])
    total = total.reshape((n, total.shape[0] // n) + total.shape[1:])
    piece = reduce_shards(layout, [total[s] for s in range(n)])
    return lax.all_gather(piece, "replica", axis=0, tiled=False)


def rolled(value, shift):
    return lax.dynamic_slice_in_dim(
        jnp.concatenate([value, value], axis=0), shift, value.shape[0], axis=0
    )


def by_shard_rows(layout, rows, chips):
    n = layout.shards
    _, _, _, shard = layout.place()
    turned = rows.T.reshape(n, chips, 2, rows.shape[1] // (2 * n * chips), rows.shape[0])
    return rolled(turned, shard).transpose(1, 2, 0, 3, 4)


def column_chunks(layout, rows):
    return rows.reshape(rows.shape[0], layout.chips, -1).transpose(1, 0, 2)


def weight_sums(layout, operands):
    normed, grad_projected, mixed, grad_attn, normed_two, grad_pre, activated, grad_branch = (
        operands
    )
    chips = layout.chips

    def flat(block):
        return block.reshape(-1, block.shape[-1])

    def pick(value, i):
        return lax.dynamic_index_in_dim(value, i, axis=0, keepdims=False)

    act_rows = by_shard_rows(layout, activated, chips)

    def down_product(chip, core):
        return jnp.dot(
            flat(pick(pick(act_rows, chip), core)), grad_branch, preferred_element_type=jnp.float32
        )

    two_rows = by_shard_rows(layout, normed_two, 1)[0]
    pre_chunks = column_chunks(layout, grad_pre)

    def up_product(chip, core):
        return jnp.dot(
            flat(pick(two_rows, core)), pick(pre_chunks, chip), preferred_element_type=jnp.float32
        )

    one_rows = by_shard_rows(layout, normed, 1)[0]
    mixed_rows = by_shard_rows(layout, mixed, 1)[0]
    first_chunks = column_chunks(layout, jnp.concatenate([grad_projected, grad_attn], axis=1))

    def first_product(chip, core):
        rows = jnp.where(chip < 3 * chips // 4, pick(one_rows, core), pick(mixed_rows, core))
        return jnp.dot(flat(rows), pick(first_chunks, chip), preferred_element_type=jnp.float32)

    down = reduce_group(layout, down_product)
    up = reduce_group(layout, up_product)
    first = reduce_group(layout, first_product)

    def columns(gathered):
        blocks = gathered.reshape((chips, 2) + gathered.shape[1:])
        blocks = blocks.transpose(1, 2, 0, 3)
        return blocks.reshape(blocks.shape[0] * blocks.shape[1], -1).astype(jnp.float32)

    first = columns(first)
    width = first.shape[1] // 4
    return (
        first[:, : 3 * width],
        first[:, 3 * width :],
        columns(up),
        flat(down).astype(jnp.float32),
    )


def solution(mesh):
    layout = Layout(mesh)

    def body(
        tokens_in,
        lengths,
        ln1_gain,
        ln1_bias,
        qkv_weight,
        query_bias,
        value_bias,
        out_weight,
        out_bias,
        ln2_gain,
        ln2_bias,
        up_weight,
        up_bias,
        down_weight,
        down_bias,
        cotangent,
    ):
        allowed = causal_mask(lengths, tokens_in.shape[0])
        layer_count = ln1_gain.shape[0]
        chips, shards = layout.chips, layout.shards
        a, b, core, shard = layout.place()
        chip = a * 2 + b

        vectors_in = (
            ln1_gain,
            ln1_bias,
            query_bias,
            value_bias,
            out_bias,
            ln2_gain,
            ln2_bias,
            up_bias,
            down_bias,
        )
        joined = lax.all_gather(jnp.concatenate(vectors_in, axis=1), "shard", axis=0, tiled=False)

        def own_columns(weight):
            rows, cols = weight.shape[0] // 2, weight.shape[1] // chips
            return lax.dynamic_slice(weight, (core * rows, chip * cols), (rows, cols))

        def own_rows(weight):
            rows = weight.shape[0] // (2 * chips)
            return lax.dynamic_slice_in_dim(weight, (chip * 2 + core) * rows, rows, axis=0)

        weights = []
        for l in range(layer_count):
            first_piece = own_columns(jnp.concatenate([qkv_weight[l], out_weight[l]], axis=1))
            first = gather_group(layout, first_piece, False)
            up = gather_group(layout, own_columns(up_weight[l]), False)
            down = gather_group(layout, own_rows(down_weight[l]), True)
            first = first.reshape(chips, -1, first.shape[-1])
            up = up.reshape(chips, -1, up.shape[-1])
            down = down.reshape(-1, down.shape[-1])
            small, at = [], 0
            for vector in vectors_in:
                size = vector.shape[1]
                small.append(joined[:, l, at : at + size].reshape(shards * size))
                at += size
            cut = 3 * chips // 4
            weights.append(
                (
                    small,
                    [first[i] for i in range(cut)],
                    [first[i] for i in range(cut, chips)],
                    [up[i] for i in range(chips)],
                    down,
                )
            )

        stream = tokens_in.astype(jnp.float32)
        saved_all = []
        for l in range(layer_count):
            stream, saved = forward_layer(stream, weights[l], allowed)
            saved_all.append(saved)
        block_out = stream.astype(jnp.bfloat16)
        grad_stream = cotangent.astype(jnp.float32)
        shares = [None] * layer_count
        for l in reversed(range(layer_count)):
            grad_stream, vectors, operands = backward_layer(
                grad_stream, weights[l], saved_all[l], allowed
            )
            sums = lax.psum(jnp.concatenate(vectors), ("replica", "shard"))
            small, at = [], 0
            for vector in vectors:
                size = vector.shape[0] // shards
                small.append(lax.dynamic_slice_in_dim(sums, at + shard * size, size))
                at += vector.shape[0]
            shares[l] = (small, weight_sums(layout, operands))

        def stacked(group, i):
            return jnp.stack([share[group][i] for share in shares])

        return (
            block_out,
            grad_stream,
            stacked(0, 0),
            stacked(0, 1),
            stacked(1, 0),
            stacked(0, 2),
            stacked(0, 3),
            stacked(1, 1),
            stacked(0, 4),
            stacked(0, 5),
            stacked(0, 6),
            stacked(1, 2),
            stacked(0, 7),
            stacked(1, 3),
            stacked(0, 8),
        )

    rows = P(("replica", "shard"), None)
    vector = P(None, "shard")
    matrix = P(None, "shard", None)
    params = (
        vector,
        vector,
        matrix,
        vector,
        vector,
        matrix,
        vector,
        vector,
        vector,
        matrix,
        vector,
        matrix,
        vector,
    )
    return jax.shard_map(
        body,
        mesh=mesh,
        in_specs=(rows, rows) + params + (rows,),
        out_specs=(rows, rows) + params,
        check_vma=False,
    )
```

```python
import functools

import jax
import jax.numpy as jnp
from jax import lax
from jax.experimental import pallas as pl
from jax.experimental.pallas import tpu as pltpu
from jax.sharding import PartitionSpec as P

HEADS = 17
HEAD = 64


norm_eps = 1e-05
score_scale = 0.125
masked_fill = -1e30


def layer_norm(values, norm_gain, norm_shift):
    center = values - jnp.mean(values, axis=-1, keepdims=True)
    spread = jnp.mean(center * center, axis=-1, keepdims=True)
    return center * lax.rsqrt(spread + norm_eps) * norm_gain + norm_shift


def gelu_tanh(values):
    return jax.nn.gelu(values, approximate=True)


def causal_mask(lengths, count):
    seq_ends = jnp.cumsum(lengths[0])
    positions = jnp.arange(count, dtype=jnp.int32)
    segment = jnp.sum((positions[:, None] >= seq_ends[None, :]).astype(jnp.int32), axis=1)
    return (segment[:, None] == segment[None, :]) & (positions[:, None] >= positions[None, :])


def split_heads(rows):
    return rows.reshape(rows.shape[0], HEADS, HEAD)


def three_parts(projected):
    width = projected.shape[1] // 3
    return (
        split_heads(projected[:, :width]),
        split_heads(projected[:, width : 2 * width]),
        split_heads(projected[:, 2 * width :]),
    )


def scores_of(queries, key_rows, allowed):
    scores = (
        jnp.einsum("qhd,khd->hqk", queries, key_rows, preferred_element_type=jnp.float32)
        * score_scale
    )
    return jnp.where(allowed[None], scores, masked_fill)


def attend(projected, allowed):
    queries, key_rows, value_rows = three_parts(projected)
    scores = scores_of(queries, key_rows, allowed)
    row_max = jnp.max(scores, axis=-1, keepdims=True)
    exponent = jnp.where(allowed[None], jnp.exp(scores - row_max), 0.0)
    totals = jnp.sum(exponent, axis=-1, keepdims=True)
    attn_probs = (exponent / totals).astype(jnp.bfloat16)
    mixed = jnp.einsum("hqk,khd->qhd", attn_probs, value_rows, preferred_element_type=jnp.float32)
    mixed = mixed.reshape(projected.shape[0], projected.shape[1] // 3)
    return (mixed.astype(jnp.bfloat16), row_max + jnp.log(totals))


def attend_back(projected, log_total, grad_mixed, allowed):
    count = projected.shape[0]
    width = projected.shape[1] // 3
    queries, key_rows, value_rows = three_parts(projected)
    grad_heads = split_heads(grad_mixed)
    scores = scores_of(queries, key_rows, allowed)
    attn_probs = jnp.where(allowed[None], jnp.exp(scores - log_total), 0.0)
    grad_values = jnp.einsum(
        "hqk,qhd->khd",
        attn_probs.astype(jnp.bfloat16),
        grad_heads,
        preferred_element_type=jnp.float32,
    )
    grad_probs = jnp.einsum(
        "qhd,khd->hqk", grad_heads, value_rows, preferred_element_type=jnp.float32
    )
    row_dot = jnp.sum(attn_probs * grad_probs, axis=-1, keepdims=True)
    grad_scores = (attn_probs * (grad_probs - row_dot)).astype(jnp.bfloat16)
    grad_queries = (
        jnp.einsum("hqk,khd->qhd", grad_scores, key_rows, preferred_element_type=jnp.float32)
        * score_scale
    )
    grad_keys = (
        jnp.einsum("hqk,qhd->khd", grad_scores, queries, preferred_element_type=jnp.float32)
        * score_scale
    )
    joined = jnp.concatenate(
        [
            grad_queries.reshape(count, width),
            grad_keys.reshape(count, width),
            grad_values.reshape(count, width),
        ],
        axis=1,
    )
    return joined.astype(jnp.bfloat16)


def dot_columns(rows, chunks):
    return jnp.concatenate(
        [jnp.dot(rows, chunk, preferred_element_type=jnp.float32) for chunk in chunks], axis=1
    )


def dot_columns_back(rows, chunks):
    width = chunks[0].shape[1]
    return sum(
        jnp.einsum(
            "te,de->td",
            rows[:, i * width : (i + 1) * width],
            chunk,
            preferred_element_type=jnp.float32,
        )
        for i, chunk in enumerate(chunks)
    )


def forward_layer(stream, weights, allowed):
    small, qkv_weight, out_weight, up_weight, down_weight = weights
    (
        norm1_gain,
        norm1_shift,
        query_bias,
        value_bias,
        out_bias,
        norm2_gain,
        norm2_shift,
        up_bias,
        down_bias,
    ) = small
    normed = layer_norm(
        stream, norm1_gain.astype(jnp.float32), norm1_shift.astype(jnp.float32)
    ).astype(jnp.bfloat16)
    qkv_bias = jnp.concatenate([query_bias, jnp.zeros_like(query_bias), value_bias]).astype(
        jnp.float32
    )
    projected = (dot_columns(normed, qkv_weight) + qkv_bias).astype(
        jnp.bfloat16
    )
    mixed, log_total = attend(projected, allowed)
    after_attn = (
        stream
        + dot_columns(mixed, out_weight)
        + out_bias.astype(jnp.float32)
    )
    normed_two = layer_norm(
        after_attn, norm2_gain.astype(jnp.float32), norm2_shift.astype(jnp.float32)
    ).astype(jnp.bfloat16)
    hidden_pre = dot_columns(normed_two, up_weight) + up_bias.astype(jnp.float32)
    activated = gelu_tanh(hidden_pre).astype(jnp.bfloat16)
    result = (
        after_attn
        + jnp.dot(activated, down_weight, preferred_element_type=jnp.float32)
        + down_bias.astype(jnp.float32)
    )
    return (
        result,
        (
            stream,
            normed,
            projected,
            mixed,
            log_total,
            after_attn,
            normed_two,
            hidden_pre,
            activated,
        ),
    )


def backward_layer(grad_out, weights, saved, allowed, layout, pipe, sum_group):
    small, qkv_weight, out_weight, up_weight, down_weight = weights
    (
        norm1_gain,
        norm1_shift,
        query_bias,
        value_bias,
        out_bias,
        norm2_gain,
        norm2_shift,
        up_bias,
        down_bias,
    ) = small
    stream, normed, projected, mixed, log_total, after_attn, normed_two, hidden_pre, activated = (
        saved
    )
    width = stream.shape[1]
    grad_branch = grad_out.astype(jnp.bfloat16)
    sum_group("down", down_product(layout, activated, grad_branch))
    grad_branch = pipe.advance(grad_branch)
    grad_down_bias = jnp.sum(grad_branch.astype(jnp.float32), axis=0)
    grad_act = jnp.einsum("td,fd->tf", grad_branch, down_weight, preferred_element_type=jnp.float32)
    gelu_value, gelu_pull = jax.vjp(gelu_tanh, hidden_pre)
    grad_pre = gelu_pull(grad_act)[0].astype(jnp.bfloat16)
    sum_group("up", up_product(layout, normed_two, grad_pre))
    grad_pre = pipe.advance(grad_pre)
    grad_up_bias = jnp.sum(grad_pre.astype(jnp.float32), axis=0)
    grad_normed_two = dot_columns_back(grad_pre, up_weight)
    norm_value, norm_pull = jax.vjp(
        layer_norm, after_attn, norm2_gain.astype(jnp.float32), norm2_shift.astype(jnp.float32)
    )
    grad_after, grad_gain_two, grad_shift_two = norm_pull(grad_normed_two)
    grad_after = grad_out + grad_after
    grad_attn = grad_after.astype(jnp.bfloat16)
    grad_out_bias = jnp.sum(grad_attn.astype(jnp.float32), axis=0)
    grad_mixed = dot_columns_back(grad_attn, out_weight).astype(jnp.bfloat16)
    grad_mixed = pipe.advance(grad_mixed)
    grad_projected = attend_back(projected, log_total, grad_mixed, allowed)
    sum_group("first", first_product(layout, normed, grad_projected, mixed, grad_attn))
    grad_projected = pipe.advance(grad_projected)
    grad_query_bias = jnp.sum(grad_projected[:, :width].astype(jnp.float32), axis=0)
    grad_value_bias = jnp.sum(grad_projected[:, 2 * width :].astype(jnp.float32), axis=0)
    grad_normed = dot_columns_back(grad_projected, qkv_weight)
    first_value, first_pull = jax.vjp(
        layer_norm, stream, norm1_gain.astype(jnp.float32), norm1_shift.astype(jnp.float32)
    )
    grad_stream, grad_gain_one, grad_shift_one = first_pull(grad_normed)
    vectors = (
        grad_gain_one,
        grad_shift_one,
        grad_query_bias,
        grad_value_bias,
        grad_out_bias,
        grad_gain_two,
        grad_shift_two,
        grad_up_bias,
        grad_down_bias,
    )
    return (grad_after + grad_stream, vectors)


class Layout:
    def __init__(self, mesh):
        self.copies = mesh.shape["replica"]
        self.shards = mesh.shape["shard"]
        self.across = self.copies // 4
        self.chips = self.copies // 2
        self.crossed = self.across == 2

    def index(self, a, b, c):
        return (a % self.across) * 4 + (b % 2) * 2 + c

    def pairs(self, way):
        out = []
        for i in range(self.copies):
            a, b, c = i // 4, (i // 2) % 2, i % 2
            turned = self.crossed and c == 1
            if way == "core":
                to = self.index(a, b, 1 - c)
            elif (way == "first") != turned:
                to = self.index(a, b + 1, c)
            else:
                to = self.index(a + 1, b, c)
            out.append((i, to))
        return out

    def move(self, value, way):
        return lax.ppermute(value, "replica", self.pairs(way))

    def place(self):
        r = lax.axis_index("replica")
        return r // 4, (r // 2) % 2, r % 2, lax.axis_index("shard")

    def chip_at(self, core, f, k):
        a, b, _, _ = self.place()
        plain = ((a + k) % self.across) * 2 + (b + f) % 2
        if not self.crossed:
            return plain
        turned = ((a + f) % self.across) * 2 + (b + k) % 2
        return jnp.where(core == 1, turned, plain)

    def slots(self):
        return [(f, k) for k in range(self.across) for f in range(2)]


def place_kernel(by_shard, index_ref, *refs):
    count = len(refs) - 2
    blocks, out_ref, sems = refs[:count], refs[count], refs[count + 1]
    shards = blocks[0].shape[0]
    copies = []
    for p in range(count):
        chip, core = index_ref[0, p], index_ref[1, p]
        for s in range(shards):
            target = out_ref.at[s, chip, core] if by_shard else out_ref.at[chip, s, core]
            copies.append(pltpu.make_async_copy(blocks[p].at[s], target, sems.at[p * shards + s]))
            copies[-1].start()
    for copy in copies:
        copy.wait()


def assemble(layout, blocks, by_shard):
    _, _, core, _ = layout.place()
    chips, shards = layout.chips, layout.shards
    own = [layout.chip_at(core, -f, -k) for f, k in layout.slots()]
    other = [layout.chip_at(1 - core, -f, -k) for f, k in layout.slots()]
    count = 2 * chips
    index = jnp.stack([jnp.stack(own + other), jnp.stack([core] * chips + [1 - core] * chips)])
    _, rows, cols = blocks[0].shape
    outer = (shards, chips) if by_shard else (chips, shards)
    return pl.pallas_call(
        functools.partial(place_kernel, by_shard),
        out_shape=jax.ShapeDtypeStruct(outer + (2, rows, cols), blocks[0].dtype),
        in_specs=[pl.BlockSpec(memory_space=pltpu.SMEM)]
        + [pl.BlockSpec(memory_space=pl.ANY)] * count,
        out_specs=pl.BlockSpec(memory_space=pltpu.VMEM),
        scratch_shapes=[pltpu.SemaphoreType.DMA((count * shards,))],
        compiler_params=pltpu.CompilerParams(vmem_limit_bytes=40 << 20),
        cost_estimate=pl.CostEstimate(
            flops=0, bytes_accessed=4 * count * shards * rows * cols, transcendentals=0
        ),
    )(index.astype(jnp.int32), *blocks)


def gather_group(layout, piece, by_shard):
    block = lax.all_gather(piece, "shard", axis=0, tiled=False)
    held = {(0, 0): block}
    held[1, 0] = layout.move(block, "first")
    for k in range(1, layout.across):
        for f in range(2):
            held[f, k] = layout.move(held[f, k - 1], "second")
    own = [held[slot] for slot in layout.slots()]
    other = [layout.move(block, "core") for block in own]
    return assemble(layout, own + other, by_shard)


def add_low(left, right):
    return (left.astype(jnp.float32) + right.astype(jnp.float32)).astype(jnp.bfloat16)


def reduce_steps(layout, product, finish):
    _, _, core, _ = layout.place()
    n, last = layout.shards, layout.across - 1
    away = {
        (f, k): product(layout.chip_at(1 - core, f, k), 1 - core).astype(jnp.bfloat16)
        for f, k in layout.slots()
    }
    came = {slot: layout.move(value, "core") for slot, value in away.items()}
    yield list(away.values())
    sums = {}
    for f, k in layout.slots():
        here = product(layout.chip_at(core, f, k), core)
        sums[f, k] = (here + came[f, k].astype(jnp.float32)).astype(jnp.bfloat16)
    totals = [sums[f, last] for f in range(2)]
    for step in range(1, layout.across):
        moved = [layout.move(total, "second") for total in totals]
        if step == 1:
            yield list(sums.values())
        totals = [add_low(moved[f], sums[f, last - step]) for f in range(2)]
    moved = layout.move(totals[1], "first")
    yield totals
    total = add_low(moved, totals[0])
    total = total.reshape((n, total.shape[0] // n) + total.shape[1:])
    piece = lax.psum_scatter(total, "shard", scatter_dimension=0, tiled=False)
    yield [total]
    moved = layout.move(piece, "first")
    yield [piece]
    held = [jnp.stack([piece, moved])]
    for _ in range(1, layout.across):
        held.append(layout.move(held[-1], "second"))
    yield [held[0]]
    own = jnp.concatenate(held, axis=0)
    other = layout.move(own, "core")
    yield [own]
    finish(jnp.concatenate([own, other], axis=0))


class Pipe:
    def __init__(self):
        self.running = []

    def begin(self, steps):
        self.running.append(steps)

    def advance(self, value):
        issued, kept = [], []
        for steps in self.running:
            try:
                issued.extend(next(steps))
                kept.append(steps)
            except StopIteration:
                pass
        self.running = kept
        return lax.optimization_barrier((value, issued))[0]

    def drain(self):
        while self.running:
            self.advance(jnp.zeros((), jnp.float32))


def by_core_rows(layout, rows, chips):
    n = layout.shards
    block = rows.T.reshape(n, chips, 2, rows.shape[1] // (2 * n * chips), rows.shape[0])
    return block.transpose(1, 2, 0, 3, 4).reshape(chips, 2, -1, rows.shape[0])


def column_chunks(layout, rows):
    return rows.reshape(rows.shape[0], layout.chips, -1).transpose(1, 0, 2)


def pick(value, i):
    return lax.dynamic_index_in_dim(value, i, axis=0, keepdims=False)


def down_product(layout, activated, grad_branch):
    rows = by_core_rows(layout, activated, layout.chips)

    def product(chip, core):
        return jnp.dot(pick(pick(rows, chip), core), grad_branch, preferred_element_type=jnp.float32)

    return product


def up_product(layout, normed_two, grad_pre):
    rows = by_core_rows(layout, normed_two, 1)[0]
    chunks = column_chunks(layout, grad_pre)

    def product(chip, core):
        return jnp.dot(pick(rows, core), pick(chunks, chip), preferred_element_type=jnp.float32)

    return product


def first_product(layout, normed, grad_projected, mixed, grad_attn):
    one_rows = by_core_rows(layout, normed, 1)[0]
    mixed_rows = by_core_rows(layout, mixed, 1)[0]
    chunks = column_chunks(layout, jnp.concatenate([grad_projected, grad_attn], axis=1))

    def product(chip, core):
        rows = jnp.where(
            chip < 3 * layout.chips // 4, pick(one_rows, core), pick(mixed_rows, core)
        )
        return jnp.dot(rows, pick(chunks, chip), preferred_element_type=jnp.float32)

    return product


def block_order(layout):
    _, _, core, _ = layout.place()
    labels = [layout.chip_at(core, -f, -k) * 2 + core for f, k in layout.slots()]
    labels += [layout.chip_at(1 - core, -f, -k) * 2 + 1 - core for f, k in layout.slots()]
    wanted = jnp.arange(len(labels), dtype=jnp.int32)
    return jnp.argmax(wanted[:, None] == jnp.stack(labels)[None, :], axis=1).astype(jnp.int32)


def sum_vectors(layout, vectors):
    n = layout.shards
    _, _, _, shard = layout.place()
    parts = jnp.concatenate([vector.reshape(n, -1) for vector in vectors], axis=1)
    total = pick(parts, (shard + n - 1) % n)
    for step in range(1, n):
        total = lax.ppermute(total, "shard", [(i, (i + 1) % n) for i in range(n)])
        total = total + pick(parts, (shard + 2 * n - 1 - step) % n)
    bit = 1
    while bit < layout.copies:
        pairs = [(i, i ^ bit) for i in range(layout.copies)]
        total = total + lax.ppermute(total, "replica", pairs)
        bit *= 2
    out, at = [], 0
    for vector in vectors:
        size = vector.shape[0] // n
        out.append(total[at : at + size])
        at += size
    return out


def write_kernel(by_rows, splits, order_ref, blocks_ref, *refs):
    outs = refs[-len(splits) :]
    chips = blocks_ref.shape[0] // 2
    rows, width = blocks_ref.shape[1:]
    if by_rows:
        for i in range(2 * chips):
            outs[0][0, i * rows : (i + 1) * rows, :] = blocks_ref[order_ref[i]].astype(jnp.float32)
        return
    for core in range(2):
        at = 0
        for out, count in zip(outs, splits):
            line = [
                blocks_ref[order_ref[2 * (at + i) + core]].astype(jnp.float32) for i in range(count)
            ]
            out[0, core * rows : (core + 1) * rows, :] = jnp.concatenate(line, axis=1)
            at += count


def write_layer(layout, whole, layer, count, by_rows, splits, held):
    blocks, rows, width = whole.shape
    if by_rows:
        shapes = [(count, blocks * rows, width)]
    else:
        shapes = [(count, 2 * rows, split * width) for split in splits]
    held = [] if held is None else held
    return pl.pallas_call(
        functools.partial(write_kernel, by_rows, splits),
        out_shape=[jax.ShapeDtypeStruct(shape, jnp.float32) for shape in shapes],
        grid=(1,),
        in_specs=[
            pl.BlockSpec(memory_space=pltpu.SMEM),
            pl.BlockSpec(whole.shape, lambda i: (0, 0, 0)),
        ]
        + [pl.BlockSpec(memory_space=pl.ANY)] * len(held),
        out_specs=[
            pl.BlockSpec((1,) + shape[1:], lambda i, layer=layer: (layer, 0, 0)) for shape in shapes
        ],
        input_output_aliases={2 + i: i for i in range(len(held))},
        compiler_params=pltpu.CompilerParams(vmem_limit_bytes=48 << 20),
        cost_estimate=pl.CostEstimate(
            flops=0, bytes_accessed=6 * blocks * rows * width, transcendentals=0
        ),
    )(block_order(layout), whole, *held)


def solution(mesh):
    layout = Layout(mesh)

    def body(
        tokens_in,
        lengths,
        ln1_gain,
        ln1_bias,
        qkv_weight,
        query_bias,
        value_bias,
        out_weight,
        out_bias,
        ln2_gain,
        ln2_bias,
        up_weight,
        up_bias,
        down_weight,
        down_bias,
        cotangent,
    ):
        allowed = causal_mask(lengths, tokens_in.shape[0])
        layer_count = ln1_gain.shape[0]
        chips, shards = layout.chips, layout.shards
        a, b, core, shard = layout.place()
        chip = a * 2 + b

        vectors_in = (
            ln1_gain,
            ln1_bias,
            query_bias,
            value_bias,
            out_bias,
            ln2_gain,
            ln2_bias,
            up_bias,
            down_bias,
        )
        joined = lax.all_gather(jnp.concatenate(vectors_in, axis=1), "shard", axis=0, tiled=False)

        def own_columns(weight):
            rows, cols = weight.shape[0] // 2, weight.shape[1] // chips
            return lax.dynamic_slice(weight, (core * rows, chip * cols), (rows, cols))

        def own_first(one, two):
            cut = 3 * chips // 4
            rows, cols = one.shape[0] // 2, one.shape[1] // cut
            from_one = lax.dynamic_slice(
                one, (core * rows, jnp.minimum(chip, cut - 1) * cols), (rows, cols)
            )
            from_two = lax.dynamic_slice(
                two, (core * rows, jnp.maximum(chip - cut, 0) * cols), (rows, cols)
            )
            return jnp.where(chip < cut, from_one, from_two)

        def own_rows(weight):
            rows = weight.shape[0] // (2 * chips)
            return lax.dynamic_slice_in_dim(weight, (chip * 2 + core) * rows, rows, axis=0)

        weights = []
        for l in range(layer_count):
            first = gather_group(layout, own_first(qkv_weight[l], out_weight[l]), False)
            up = gather_group(layout, own_columns(up_weight[l]), False)
            down = gather_group(layout, own_rows(down_weight[l]), True)
            first = first.reshape(chips, -1, first.shape[-1])
            up = up.reshape(chips, -1, up.shape[-1])
            down = down.reshape(-1, down.shape[-1])
            small, at = [], 0
            for vector in vectors_in:
                size = vector.shape[1]
                small.append(joined[:, l, at : at + size].reshape(shards * size))
                at += size
            cut = 3 * chips // 4
            weights.append(
                (
                    small,
                    [first[i] for i in range(cut)],
                    [first[i] for i in range(cut, chips)],
                    [up[i] for i in range(chips)],
                    down,
                )
            )

        stream = tokens_in.astype(jnp.float32)
        saved_all = []
        for l in range(layer_count):
            stream, saved = forward_layer(stream, weights[l], allowed)
            saved_all.append(saved)
        block_out = stream.astype(jnp.bfloat16)
        grad_stream = cotangent.astype(jnp.float32)
        shares = [None] * layer_count
        pipe = Pipe()
        held = {"first": None, "up": None, "down": None}

        def sum_group(name, l, product):
            cut = 3 * chips // 4
            splits = (cut, chips - cut) if name == "first" else (chips,)

            def finish(whole):
                held[name] = write_layer(
                    layout, whole, l, layer_count, name == "down", splits, held[name]
                )

            pipe.begin(reduce_steps(layout, product, finish))

        for l in reversed(range(layer_count)):
            grad_stream, vectors = backward_layer(
                grad_stream,
                weights[l],
                saved_all[l],
                allowed,
                layout,
                pipe,
                lambda name, product, l=l: sum_group(name, l, product),
            )
            shares[l] = sum_vectors(layout, vectors)
        pipe.drain()

        def stacked(i):
            return jnp.stack([share[i] for share in shares])

        return (
            block_out,
            grad_stream,
            stacked(0),
            stacked(1),
            held["first"][0],
            stacked(2),
            stacked(3),
            held["first"][1],
            stacked(4),
            stacked(5),
            stacked(6),
            held["up"][0],
            stacked(7),
            held["down"][0],
            stacked(8),
        )

    rows = P(("replica", "shard"), None)
    vector = P(None, "shard")
    matrix = P(None, "shard", None)
    params = (
        vector,
        vector,
        matrix,
        vector,
        vector,
        matrix,
        vector,
        vector,
        vector,
        matrix,
        vector,
        matrix,
        vector,
    )
    return jax.shard_map(
        body,
        mesh=mesh,
        in_specs=(rows, rows) + params + (rows,),
        out_specs=(rows, rows) + params,
        check_vma=False,
    )
```

```python
import functools

import jax
import jax.numpy as jnp
from jax import lax
from jax.experimental import pallas as pl
from jax.experimental.pallas import tpu as pltpu
from jax.sharding import PartitionSpec as P

HEADS = 17
HEAD = 64


norm_eps = 1e-05
score_scale = 0.125
masked_fill = -1e30


def layer_norm(values, norm_gain, norm_shift):
    center = values - jnp.mean(values, axis=-1, keepdims=True)
    spread = jnp.mean(center * center, axis=-1, keepdims=True)
    return center * lax.rsqrt(spread + norm_eps) * norm_gain + norm_shift


def gelu_tanh(values):
    return jax.nn.gelu(values, approximate=True)


def sequence_starts(lengths, count):
    seq_ends = jnp.cumsum(lengths[0])
    positions = jnp.arange(count, dtype=jnp.int32)
    passed = positions[:, None] >= seq_ends[None, :]
    return jnp.max(jnp.where(passed, seq_ends[None, :], 0), axis=1, keepdims=True)


def rows_at_once(count):
    return 256 if count % 256 == 0 else count


def mask_add(starts_ref, first, rows, keys):
    at = lax.broadcasted_iota(jnp.int32, (rows, keys), 0) + first
    key = lax.broadcasted_iota(jnp.int32, (rows, keys), 1)
    allowed = (key <= at) & (key >= starts_ref[first : first + rows, :])
    return jnp.where(allowed, 0.0, masked_fill)


def across(left, right):
    return lax.dot_general(
        left, right, (((1,), (1,)), ((), ())), preferred_element_type=jnp.float32
    )


def down(left, right):
    return lax.dot_general(
        left, right, (((0,), (0,)), ((), ())), preferred_element_type=jnp.float32
    )


def over_heads(step):
    def pair(i, _):
        step(pl.multiple_of(i * 2 * HEAD, 2 * HEAD), 2, i)
        return 0

    lax.fori_loop(0, HEADS // 2, pair, 0)
    if HEADS % 2:
        step((HEADS - 1) * HEAD, 1, HEADS // 2)


def side_by_side(parts):
    return parts[0] if len(parts) == 1 else jnp.concatenate(parts, axis=1)


def attend_kernel(starts_ref, q_ref, k_ref, v_ref, mixed_ref, log_ref):
    count = q_ref.shape[0]
    rows = rows_at_once(count)
    for first in range(0, count, rows):
        keys = first + rows
        mask = mask_add(starts_ref, first, rows, keys)

        def step(at, heads, pair, first=first, keys=keys, mask=mask):
            cols = pl.ds(at, heads * HEAD)
            queries = q_ref[first:keys, cols]
            key_rows = k_ref[0:keys, cols]
            value_rows = v_ref[0:keys, cols]
            mixed = []
            for h in range(heads):
                own = slice(h * HEAD, (h + 1) * HEAD)
                scores = across(queries[:, own], key_rows[:, own]) * score_scale + mask
                row_max = jnp.max(scores, axis=1, keepdims=True)
                exponent = jnp.exp(scores - row_max)
                totals = jnp.sum(exponent, axis=1, keepdims=True)
                probs = (exponent * (1.0 / totals)).astype(jnp.bfloat16)
                mixed.append(
                    jnp.dot(probs, value_rows[:, own], preferred_element_type=jnp.float32)
                )
                log_ref[pair * 2 + h, first:keys, :] = row_max + jnp.log(totals)
            mixed_ref[first:keys, cols] = side_by_side(mixed).astype(jnp.bfloat16)

        over_heads(step)


def attend(queries, key_rows, value_rows, starts):
    count, width = queries.shape
    return pl.pallas_call(
        attend_kernel,
        out_shape=(
            jax.ShapeDtypeStruct((count, width), jnp.bfloat16),
            jax.ShapeDtypeStruct((HEADS, count, 1), jnp.float32),
        ),
        compiler_params=pltpu.CompilerParams(vmem_limit_bytes=48 << 20),
        cost_estimate=pl.CostEstimate(
            flops=4 * count * count * width,
            bytes_accessed=8 * count * width,
            transcendentals=HEADS * count * count,
        ),
    )(starts, queries, key_rows, value_rows)


def attend_back_kernel(
    starts_ref, q_ref, k_ref, v_ref, log_ref, g_ref, gq_ref, gk_ref, gv_ref, key_sum, value_sum
):
    count = q_ref.shape[0]
    rows = rows_at_once(count)
    masks = [mask_add(starts_ref, first, rows, first + rows) for first in range(0, count, rows)]

    def step(at, heads, pair):
        cols = pl.ds(at, heads * HEAD)
        key_sum[...] = jnp.zeros_like(key_sum)
        value_sum[...] = jnp.zeros_like(value_sum)
        for first, mask in zip(range(0, count, rows), masks):
            keys = first + rows
            queries, grads = q_ref[first:keys, cols], g_ref[first:keys, cols]
            key_rows, value_rows = k_ref[0:keys, cols], v_ref[0:keys, cols]
            query_parts, key_parts, value_parts = [], [], []
            for h in range(heads):
                own = slice(h * HEAD, (h + 1) * HEAD)
                scores = across(queries[:, own], key_rows[:, own]) * score_scale + mask
                probs = jnp.exp(scores - log_ref[pair * 2 + h, first:keys, :])
                value_parts.append(down(probs.astype(jnp.bfloat16), grads[:, own]))
                grad_probs = across(grads[:, own], value_rows[:, own])
                row_dot = jnp.sum(probs * grad_probs, axis=1, keepdims=True)
                grad_scores = (probs * (grad_probs - row_dot)).astype(jnp.bfloat16)
                query_parts.append(
                    jnp.dot(grad_scores, key_rows[:, own], preferred_element_type=jnp.float32)
                )
                key_parts.append(down(grad_scores, queries[:, own]))
            width = heads * HEAD
            gq_ref[first:keys, cols] = (side_by_side(query_parts) * score_scale).astype(
                jnp.bfloat16
            )
            key_sum[0:keys, 0:width] += side_by_side(key_parts)
            value_sum[0:keys, 0:width] += side_by_side(value_parts)
        width = heads * HEAD
        gk_ref[:, cols] = (key_sum[:, 0:width] * score_scale).astype(jnp.bfloat16)
        gv_ref[:, cols] = value_sum[:, 0:width].astype(jnp.bfloat16)

    over_heads(step)


def attend_back(queries, key_rows, value_rows, log_total, grad_mixed, starts):
    count, width = queries.shape
    shape = jax.ShapeDtypeStruct((count, width), jnp.bfloat16)
    return pl.pallas_call(
        attend_back_kernel,
        out_shape=(shape, shape, shape),
        scratch_shapes=[pltpu.VMEM((count, 2 * HEAD), jnp.float32)] * 2,
        compiler_params=pltpu.CompilerParams(vmem_limit_bytes=48 << 20),
        cost_estimate=pl.CostEstimate(
            flops=10 * count * count * width,
            bytes_accessed=14 * count * width,
            transcendentals=HEADS * count * count,
        ),
    )(starts, queries, key_rows, value_rows, log_total, grad_mixed)


def dot_columns(rows, chunks):
    return jnp.concatenate(
        [jnp.dot(rows, chunk, preferred_element_type=jnp.float32) for chunk in chunks], axis=1
    )


def dot_columns_back(rows, chunks):
    width = chunks[0].shape[1]
    return sum(
        jnp.einsum(
            "te,de->td",
            rows[:, i * width : (i + 1) * width],
            chunk,
            preferred_element_type=jnp.float32,
        )
        for i, chunk in enumerate(chunks)
    )


def forward_layer(stream, weights, starts, layout):
    small, qkv_weight, out_weight, up_weight, down_weight = weights
    (
        norm1_gain,
        norm1_shift,
        query_bias,
        value_bias,
        out_bias,
        norm2_gain,
        norm2_shift,
        up_bias,
        down_bias,
    ) = small
    normed = layer_norm(
        stream, norm1_gain.astype(jnp.float32), norm1_shift.astype(jnp.float32)
    ).astype(jnp.bfloat16)
    joined = dot_columns(normed, qkv_weight)
    width = stream.shape[1]
    queries = (joined[:, :width] + query_bias.astype(jnp.float32)).astype(jnp.bfloat16)
    key_rows = joined[:, width : 2 * width].astype(jnp.bfloat16)
    value_rows = (joined[:, 2 * width :] + value_bias.astype(jnp.float32)).astype(jnp.bfloat16)
    projected = (queries, key_rows, value_rows)
    mixed, log_total = attend(queries, key_rows, value_rows, starts)
    after_attn = (
        stream
        + dot_columns(mixed, out_weight)
        + out_bias.astype(jnp.float32)
    )
    normed_two = layer_norm(
        after_attn, norm2_gain.astype(jnp.float32), norm2_shift.astype(jnp.float32)
    ).astype(jnp.bfloat16)
    hidden_pre = dot_columns(normed_two, up_weight) + up_bias.astype(jnp.float32)
    activated = gelu_tanh(hidden_pre).astype(jnp.bfloat16)
    result = (
        after_attn
        + jnp.dot(activated, down_weight, preferred_element_type=jnp.float32)
        + down_bias.astype(jnp.float32)
    )
    return (
        result,
        (
            stream,
            normed,
            projected,
            mixed,
            log_total,
            after_attn,
            normed_two,
            hidden_pre,
            activated,
        ),
    )


def backward_layer(grad_out, weights, saved, starts, layout, pipe, sum_group):
    small, qkv_weight, out_weight, up_weight, down_weight = weights
    (
        norm1_gain,
        norm1_shift,
        query_bias,
        value_bias,
        out_bias,
        norm2_gain,
        norm2_shift,
        up_bias,
        down_bias,
    ) = small
    stream, normed, projected, mixed, log_total, after_attn, normed_two, hidden_pre, activated = (
        saved
    )
    grad_branch = grad_out.astype(jnp.bfloat16)
    sum_group("down", down_product(layout, activated, grad_branch))
    grad_branch = pipe.advance(grad_branch)
    grad_down_bias = jnp.sum(grad_branch.astype(jnp.float32), axis=0)
    grad_act = jnp.einsum("td,fd->tf", grad_branch, down_weight, preferred_element_type=jnp.float32)
    gelu_value, gelu_pull = jax.vjp(gelu_tanh, hidden_pre)
    grad_pre = gelu_pull(grad_act)[0].astype(jnp.bfloat16)
    sum_group("up", up_product(layout, normed_two, grad_pre))
    grad_pre = pipe.advance(grad_pre)
    grad_up_bias = jnp.sum(grad_pre.astype(jnp.float32), axis=0)
    grad_normed_two = dot_columns_back(grad_pre, up_weight)
    norm_value, norm_pull = jax.vjp(
        layer_norm, after_attn, norm2_gain.astype(jnp.float32), norm2_shift.astype(jnp.float32)
    )
    grad_after, grad_gain_two, grad_shift_two = norm_pull(grad_normed_two)
    grad_after = grad_out + grad_after
    grad_attn = grad_after.astype(jnp.bfloat16)
    grad_out_bias = jnp.sum(grad_attn.astype(jnp.float32), axis=0)
    grad_mixed = dot_columns_back(grad_attn, out_weight).astype(jnp.bfloat16)
    grad_mixed = pipe.advance(grad_mixed)
    thirds = attend_back(*projected, log_total, grad_mixed, starts)
    sum_group("first", first_product(layout, normed, thirds, mixed, grad_attn))
    thirds = pipe.advance(thirds)
    grad_query_bias = jnp.sum(thirds[0].astype(jnp.float32), axis=0)
    grad_value_bias = jnp.sum(thirds[2].astype(jnp.float32), axis=0)
    if len(qkv_weight) == 3:
        pieces = list(thirds)
    else:
        cols = qkv_weight[0].shape[1]
        whole = jnp.concatenate(thirds, axis=1)
        pieces = [whole[:, i * cols : (i + 1) * cols] for i in range(len(qkv_weight))]
    grad_normed = sum(
        jnp.einsum("te,de->td", piece, chunk, preferred_element_type=jnp.float32)
        for piece, chunk in zip(pieces, qkv_weight)
    )
    first_value, first_pull = jax.vjp(
        layer_norm, stream, norm1_gain.astype(jnp.float32), norm1_shift.astype(jnp.float32)
    )
    grad_stream, grad_gain_one, grad_shift_one = first_pull(grad_normed)
    vectors = (
        grad_gain_one,
        grad_shift_one,
        grad_query_bias,
        grad_value_bias,
        grad_out_bias,
        grad_gain_two,
        grad_shift_two,
        grad_up_bias,
        grad_down_bias,
    )
    return (grad_after + grad_stream, vectors)


class Layout:
    def __init__(self, mesh):
        self.copies = mesh.shape["replica"]
        self.shards = mesh.shape["shard"]
        self.across = self.copies // 4
        self.chips = self.copies // 2
        self.crossed = self.across == 2

    def index(self, a, b, c):
        return (a % self.across) * 4 + (b % 2) * 2 + c

    def pairs(self, way):
        out = []
        for i in range(self.copies):
            a, b, c = i // 4, (i // 2) % 2, i % 2
            turned = self.crossed and c == 1
            if way == "core":
                to = self.index(a, b, 1 - c)
            elif (way == "first") != turned:
                to = self.index(a, b + 1, c)
            else:
                to = self.index(a + 1, b, c)
            out.append((i, to))
        return out

    def move(self, value, way):
        return lax.ppermute(value, "replica", self.pairs(way))

    def place(self):
        r = lax.axis_index("replica")
        return r // 4, (r // 2) % 2, r % 2, lax.axis_index("shard")

    def chip_at(self, core, f, k):
        a, b, _, _ = self.place()
        plain = ((a + k) % self.across) * 2 + (b + f) % 2
        if not self.crossed:
            return plain
        turned = ((a + f) % self.across) * 2 + (b + k) % 2
        return jnp.where(core == 1, turned, plain)

    def slots(self):
        return [(f, k) for k in range(self.across) for f in range(2)]


def place_kernel(by_shard, index_ref, *refs):
    count = len(refs) - 2
    blocks, out_ref, sems = refs[:count], refs[count], refs[count + 1]
    shards = blocks[0].shape[0]
    copies = []
    for p in range(count):
        chip, core = index_ref[0, p], index_ref[1, p]
        for s in range(shards):
            target = out_ref.at[s, chip, core] if by_shard else out_ref.at[chip, s, core]
            copies.append(pltpu.make_async_copy(blocks[p].at[s], target, sems.at[p * shards + s]))
            copies[-1].start()
    for copy in copies:
        copy.wait()


def assemble(layout, blocks, by_shard):
    _, _, core, _ = layout.place()
    chips, shards = layout.chips, layout.shards
    own = [layout.chip_at(core, -f, -k) for f, k in layout.slots()]
    other = [layout.chip_at(1 - core, -f, -k) for f, k in layout.slots()]
    count = 2 * chips
    index = jnp.stack([jnp.stack(own + other), jnp.stack([core] * chips + [1 - core] * chips)])
    _, rows, cols = blocks[0].shape
    outer = (shards, chips) if by_shard else (chips, shards)
    return pl.pallas_call(
        functools.partial(place_kernel, by_shard),
        out_shape=jax.ShapeDtypeStruct(outer + (2, rows, cols), blocks[0].dtype),
        in_specs=[pl.BlockSpec(memory_space=pltpu.SMEM)]
        + [pl.BlockSpec(memory_space=pl.ANY)] * count,
        out_specs=pl.BlockSpec(memory_space=pltpu.VMEM),
        scratch_shapes=[pltpu.SemaphoreType.DMA((count * shards,))],
        compiler_params=pltpu.CompilerParams(vmem_limit_bytes=40 << 20),
        cost_estimate=pl.CostEstimate(
            flops=0, bytes_accessed=4 * count * shards * rows * cols, transcendentals=0
        ),
    )(index.astype(jnp.int32), *blocks)


def gather_group(layout, piece, by_shard, before):
    block = lax.all_gather(piece, "shard", axis=0, tiled=False)
    if before is not None:
        block = lax.optimization_barrier((block, before[0]))[0]
    moved = layout.move(block, "first")
    starts = (block, moved)
    if before is not None:
        starts = lax.optimization_barrier((starts, before[1]))[0]
    held = {(0, 0): starts[0], (1, 0): starts[1]}
    for k in range(1, layout.across):
        for f in range(2):
            held[f, k] = layout.move(held[f, k - 1], "second")
    own = [held[slot] for slot in layout.slots()]
    other = [layout.move(block, "core") for block in own]
    return assemble(layout, own + other, by_shard), (moved, own[2:])


def add_low(left, right):
    return (left.astype(jnp.float32) + right.astype(jnp.float32)).astype(jnp.bfloat16)


def reduce_steps(layout, product, finish):
    _, _, core, _ = layout.place()
    n, last = layout.shards, layout.across - 1
    away = {
        (f, k): product(layout.chip_at(1 - core, f, k), 1 - core).astype(jnp.bfloat16)
        for f, k in layout.slots()
    }
    came = {slot: layout.move(value, "core") for slot, value in away.items()}
    yield list(away.values())
    sums = {}
    for f, k in layout.slots():
        here = product(layout.chip_at(core, f, k), core)
        sums[f, k] = (here + came[f, k].astype(jnp.float32)).astype(jnp.bfloat16)
    totals = [sums[f, last] for f in range(2)]
    for step in range(1, layout.across):
        moved = [layout.move(total, "second") for total in totals]
        if step == 1:
            yield list(sums.values())
        totals = [add_low(moved[f], sums[f, last - step]) for f in range(2)]
    moved = layout.move(totals[1], "first")
    yield totals
    total = add_low(moved, totals[0])
    total = total.reshape((n, total.shape[0] // n) + total.shape[1:])
    piece = lax.psum_scatter(total, "shard", scatter_dimension=0, tiled=False)
    yield [total]
    moved = layout.move(piece, "first")
    yield [piece]
    held = [jnp.stack([piece, moved])]
    for _ in range(1, layout.across):
        held.append(layout.move(held[-1], "second"))
    yield [held[0]]
    own = jnp.concatenate(held, axis=0)
    other = layout.move(own, "core")
    yield [own]
    finish(jnp.concatenate([own, other], axis=0))


class Pipe:
    def __init__(self):
        self.running = []

    def begin(self, steps):
        self.running.append(steps)

    def advance(self, value):
        issued, kept = [], []
        for steps in self.running:
            try:
                issued.extend(next(steps))
                kept.append(steps)
            except StopIteration:
                pass
        self.running = kept
        return lax.optimization_barrier((value, issued))[0]

    def drain(self):
        while self.running:
            self.advance(jnp.zeros((), jnp.float32))


def by_core_rows(layout, rows, chips):
    n = layout.shards
    block = rows.T.reshape(n, chips, 2, rows.shape[1] // (2 * n * chips), rows.shape[0])
    return block.transpose(1, 2, 0, 3, 4).reshape(chips, 2, -1, rows.shape[0])


def column_chunks(layout, rows):
    return rows.reshape(rows.shape[0], layout.chips, -1).transpose(1, 0, 2)


def pick(value, i):
    return lax.dynamic_index_in_dim(value, i, axis=0, keepdims=False)


def down_product(layout, activated, grad_branch):
    rows = by_core_rows(layout, activated, layout.chips)

    def product(chip, core):
        return jnp.dot(pick(pick(rows, chip), core), grad_branch, preferred_element_type=jnp.float32)

    return product


def up_product(layout, normed_two, grad_pre):
    rows = by_core_rows(layout, normed_two, 1)[0]
    chunks = column_chunks(layout, grad_pre)

    def product(chip, core):
        return jnp.dot(pick(rows, core), pick(chunks, chip), preferred_element_type=jnp.float32)

    return product


def first_product(layout, normed, thirds, mixed, grad_attn):
    one_rows = by_core_rows(layout, normed, 1)[0]
    mixed_rows = by_core_rows(layout, mixed, 1)[0]
    if layout.chips == 4:
        chunks = jnp.stack(list(thirds) + [grad_attn])
    else:
        chunks = column_chunks(layout, jnp.concatenate(list(thirds) + [grad_attn], axis=1))

    def product(chip, core):
        rows = jnp.where(
            chip < 3 * layout.chips // 4, pick(one_rows, core), pick(mixed_rows, core)
        )
        return jnp.dot(rows, pick(chunks, chip), preferred_element_type=jnp.float32)

    return product


def block_order(layout):
    _, _, core, _ = layout.place()
    labels = [layout.chip_at(core, -f, -k) * 2 + core for f, k in layout.slots()]
    labels += [layout.chip_at(1 - core, -f, -k) * 2 + 1 - core for f, k in layout.slots()]
    wanted = jnp.arange(len(labels), dtype=jnp.int32)
    return jnp.argmax(wanted[:, None] == jnp.stack(labels)[None, :], axis=1).astype(jnp.int32)


def sum_vectors(layout, vectors):
    n = layout.shards
    _, _, _, shard = layout.place()
    parts = jnp.concatenate([vector.reshape(n, -1) for vector in vectors], axis=1)
    total = pick(parts, (shard + n - 1) % n)
    for step in range(1, n):
        total = lax.ppermute(total, "shard", [(i, (i + 1) % n) for i in range(n)])
        total = total + pick(parts, (shard + 2 * n - 1 - step) % n)
    bit = 1
    while bit < layout.copies:
        pairs = [(i, i ^ bit) for i in range(layout.copies)]
        total = total + lax.ppermute(total, "replica", pairs)
        bit *= 2
    out, at = [], 0
    for vector in vectors:
        size = vector.shape[0] // n
        out.append(total[at : at + size])
        at += size
    return out


def write_kernel(by_rows, splits, order_ref, blocks_ref, *refs):
    outs = refs[-len(splits) :]
    chips = blocks_ref.shape[0] // 2
    rows, width = blocks_ref.shape[1:]
    if by_rows:
        for i in range(2 * chips):
            outs[0][0, i * rows : (i + 1) * rows, :] = blocks_ref[order_ref[i]].astype(jnp.float32)
        return
    for core in range(2):
        at = 0
        for out, count in zip(outs, splits):
            line = [
                blocks_ref[order_ref[2 * (at + i) + core]].astype(jnp.float32) for i in range(count)
            ]
            out[0, core * rows : (core + 1) * rows, :] = jnp.concatenate(line, axis=1)
            at += count


def write_layer(layout, whole, layer, count, by_rows, splits, held):
    blocks, rows, width = whole.shape
    if by_rows:
        shapes = [(count, blocks * rows, width)]
    else:
        shapes = [(count, 2 * rows, split * width) for split in splits]
    held = [] if held is None else held
    return pl.pallas_call(
        functools.partial(write_kernel, by_rows, splits),
        out_shape=[jax.ShapeDtypeStruct(shape, jnp.float32) for shape in shapes],
        grid=(1,),
        in_specs=[
            pl.BlockSpec(memory_space=pltpu.SMEM),
            pl.BlockSpec(whole.shape, lambda i: (0, 0, 0)),
        ]
        + [pl.BlockSpec(memory_space=pl.ANY)] * len(held),
        out_specs=[
            pl.BlockSpec((1,) + shape[1:], lambda i, layer=layer: (layer, 0, 0)) for shape in shapes
        ],
        input_output_aliases={2 + i: i for i in range(len(held))},
        compiler_params=pltpu.CompilerParams(vmem_limit_bytes=48 << 20),
        cost_estimate=pl.CostEstimate(
            flops=0, bytes_accessed=6 * blocks * rows * width, transcendentals=0
        ),
    )(block_order(layout), whole, *held)


def solution(mesh):
    layout = Layout(mesh)

    def body(
        tokens_in,
        lengths,
        ln1_gain,
        ln1_bias,
        qkv_weight,
        query_bias,
        value_bias,
        out_weight,
        out_bias,
        ln2_gain,
        ln2_bias,
        up_weight,
        up_bias,
        down_weight,
        down_bias,
        cotangent,
    ):
        starts = sequence_starts(lengths, tokens_in.shape[0])
        layer_count = ln1_gain.shape[0]
        chips, shards = layout.chips, layout.shards
        a, b, core, shard = layout.place()
        chip = a * 2 + b

        vectors_in = (
            ln1_gain,
            ln1_bias,
            query_bias,
            value_bias,
            out_bias,
            ln2_gain,
            ln2_bias,
            up_bias,
            down_bias,
        )
        joined = lax.all_gather(jnp.concatenate(vectors_in, axis=1), "shard", axis=0, tiled=False)

        def own_columns(weight):
            rows, cols = weight.shape[0] // 2, weight.shape[1] // chips
            return lax.dynamic_slice(weight, (core * rows, chip * cols), (rows, cols))

        def own_first(one, two):
            cut = 3 * chips // 4
            rows, cols = one.shape[0] // 2, one.shape[1] // cut
            from_one = lax.dynamic_slice(
                one, (core * rows, jnp.minimum(chip, cut - 1) * cols), (rows, cols)
            )
            from_two = lax.dynamic_slice(
                two, (core * rows, jnp.maximum(chip - cut, 0) * cols), (rows, cols)
            )
            return jnp.where(chip < cut, from_one, from_two)

        def own_rows(weight):
            rows = weight.shape[0] // (2 * chips)
            return lax.dynamic_slice_in_dim(weight, (chip * 2 + core) * rows, rows, axis=0)

        weights, before = [], None
        for l in range(layer_count):
            first, before = gather_group(
                layout, own_first(qkv_weight[l], out_weight[l]), False, before
            )
            up, before = gather_group(layout, own_columns(up_weight[l]), False, before)
            down, before = gather_group(layout, own_rows(down_weight[l]), True, before)
            first = first.reshape(chips, -1, first.shape[-1])
            up = up.reshape(chips, -1, up.shape[-1])
            down = down.reshape(-1, down.shape[-1])
            small, at = [], 0
            for vector in vectors_in:
                size = vector.shape[1]
                small.append(joined[:, l, at : at + size].reshape(shards * size))
                at += size
            cut = 3 * chips // 4
            weights.append(
                (
                    small,
                    [first[i] for i in range(cut)],
                    [first[i] for i in range(cut, chips)],
                    [up[i] for i in range(chips)],
                    down,
                )
            )

        stream = tokens_in.astype(jnp.float32)
        saved_all = []
        for l in range(layer_count):
            stream, saved = forward_layer(stream, weights[l], starts, layout)
            saved_all.append(saved)
        block_out = stream.astype(jnp.bfloat16)
        grad_stream = cotangent.astype(jnp.float32)
        shares = [None] * layer_count
        pipe = Pipe()
        held = {"first": None, "up": None, "down": None}

        def sum_group(name, l, product):
            cut = 3 * chips // 4
            splits = (cut, chips - cut) if name == "first" else (chips,)

            def finish(whole):
                held[name] = write_layer(
                    layout, whole, l, layer_count, name == "down", splits, held[name]
                )

            pipe.begin(reduce_steps(layout, product, finish))

        for l in reversed(range(layer_count)):
            grad_stream, vectors = backward_layer(
                grad_stream,
                weights[l],
                saved_all[l],
                starts,
                layout,
                pipe,
                lambda name, product, l=l: sum_group(name, l, product),
            )
            shares[l] = sum_vectors(layout, vectors)
        pipe.drain()

        def stacked(i):
            return jnp.stack([share[i] for share in shares])

        return (
            block_out,
            grad_stream,
            stacked(0),
            stacked(1),
            held["first"][0],
            stacked(2),
            stacked(3),
            held["first"][1],
            stacked(4),
            stacked(5),
            stacked(6),
            held["up"][0],
            stacked(7),
            held["down"][0],
            stacked(8),
        )

    rows = P(("replica", "shard"), None)
    vector = P(None, "shard")
    matrix = P(None, "shard", None)
    params = (
        vector,
        vector,
        matrix,
        vector,
        vector,
        matrix,
        vector,
        vector,
        vector,
        matrix,
        vector,
        matrix,
        vector,
    )
    return jax.shard_map(
        body,
        mesh=mesh,
        in_specs=(rows, rows) + params + (rows,),
        out_specs=(rows, rows) + params,
        check_vma=False,
    )
```

```python
import functools

import jax
import jax.numpy as jnp
from jax import lax
from jax.experimental import pallas as pl
from jax.experimental.pallas import tpu as pltpu
from jax.sharding import PartitionSpec as P

HEADS = 17
HEAD = 64


norm_eps = 1e-05
score_scale = 0.125
masked_fill = -1e30


def layer_norm(values, norm_gain, norm_shift):
    center = values - jnp.mean(values, axis=-1, keepdims=True)
    spread = jnp.mean(center * center, axis=-1, keepdims=True)
    return center * lax.rsqrt(spread + norm_eps) * norm_gain + norm_shift


def gelu_and_slope(values):
    inner = 0.7978845608028654 * (values + 0.044715 * values * values * values)
    bend = jnp.tanh(inner)
    value = 0.5 * values * (1.0 + bend)
    rate = 0.7978845608028654 * (1.0 + 0.134145 * values * values)
    slope = 0.5 * (1.0 + bend) + 0.5 * values * (1.0 - bend * bend) * rate
    return value, slope


def sequence_starts(lengths, count):
    seq_ends = jnp.cumsum(lengths[0])
    positions = jnp.arange(count, dtype=jnp.int32)
    passed = positions[:, None] >= seq_ends[None, :]
    return jnp.max(jnp.where(passed, seq_ends[None, :], 0), axis=1, keepdims=True)


def rows_at_once(count):
    return 256 if count % 256 == 0 else count


def mask_add(starts_ref, first, rows, keys):
    at = lax.broadcasted_iota(jnp.int32, (rows, keys), 0) + first
    key = lax.broadcasted_iota(jnp.int32, (rows, keys), 1)
    allowed = (key <= at) & (key >= starts_ref[first : first + rows, :])
    return jnp.where(allowed, 0.0, masked_fill)


def across(left, right):
    return lax.dot_general(
        left, right, (((1,), (1,)), ((), ())), preferred_element_type=jnp.float32
    )


def down(left, right):
    return lax.dot_general(
        left, right, (((0,), (0,)), ((), ())), preferred_element_type=jnp.float32
    )


def over_heads(step):
    def pair(i, _):
        step(pl.multiple_of(i * 2 * HEAD, 2 * HEAD), 2, i)
        return 0

    lax.fori_loop(0, HEADS // 2, pair, 0)
    if HEADS % 2:
        step((HEADS - 1) * HEAD, 1, HEADS // 2)


def side_by_side(parts):
    return parts[0] if len(parts) == 1 else jnp.concatenate(parts, axis=1)


def attend_kernel(starts_ref, q_ref, k_ref, v_ref, mixed_ref, log_ref):
    count = q_ref.shape[0]
    rows = rows_at_once(count)
    for first in range(0, count, rows):
        keys = first + rows
        mask = mask_add(starts_ref, first, rows, keys)

        def step(at, heads, pair, first=first, keys=keys, mask=mask):
            cols = pl.ds(at, heads * HEAD)
            queries = q_ref[first:keys, cols]
            key_rows = k_ref[0:keys, cols]
            value_rows = v_ref[0:keys, cols]
            mixed = []
            for h in range(heads):
                own = slice(h * HEAD, (h + 1) * HEAD)
                scores = across(queries[:, own], key_rows[:, own]) * score_scale + mask
                row_max = jnp.max(scores, axis=1, keepdims=True)
                exponent = jnp.exp(scores - row_max)
                totals = jnp.sum(exponent, axis=1, keepdims=True)
                probs = (exponent * (1.0 / totals)).astype(jnp.bfloat16)
                mixed.append(
                    jnp.dot(probs, value_rows[:, own], preferred_element_type=jnp.float32)
                )
                log_ref[pair * 2 + h, first:keys, :] = row_max + jnp.log(totals)
            mixed_ref[first:keys, cols] = side_by_side(mixed).astype(jnp.bfloat16)

        over_heads(step)


def attend(queries, key_rows, value_rows, starts):
    count, width = queries.shape
    return pl.pallas_call(
        attend_kernel,
        out_shape=(
            jax.ShapeDtypeStruct((count, width), jnp.bfloat16),
            jax.ShapeDtypeStruct((HEADS, count, 1), jnp.float32),
        ),
        compiler_params=pltpu.CompilerParams(vmem_limit_bytes=48 << 20),
        cost_estimate=pl.CostEstimate(
            flops=4 * count * count * width,
            bytes_accessed=8 * count * width,
            transcendentals=HEADS * count * count,
        ),
    )(starts, queries, key_rows, value_rows)


def attend_back_kernel(
    starts_ref, q_ref, k_ref, v_ref, log_ref, g_ref, gq_ref, gk_ref, gv_ref, key_sum, value_sum
):
    count = q_ref.shape[0]
    rows = rows_at_once(count)
    masks = [mask_add(starts_ref, first, rows, first + rows) for first in range(0, count, rows)]

    def step(at, heads, pair):
        cols = pl.ds(at, heads * HEAD)
        key_sum[...] = jnp.zeros_like(key_sum)
        value_sum[...] = jnp.zeros_like(value_sum)
        for first, mask in zip(range(0, count, rows), masks):
            keys = first + rows
            queries, grads = q_ref[first:keys, cols], g_ref[first:keys, cols]
            key_rows, value_rows = k_ref[0:keys, cols], v_ref[0:keys, cols]
            query_parts, key_parts, value_parts = [], [], []
            for h in range(heads):
                own = slice(h * HEAD, (h + 1) * HEAD)
                scores = across(queries[:, own], key_rows[:, own]) * score_scale + mask
                probs = jnp.exp(scores - log_ref[pair * 2 + h, first:keys, :])
                value_parts.append(down(probs.astype(jnp.bfloat16), grads[:, own]))
                grad_probs = across(grads[:, own], value_rows[:, own])
                row_dot = jnp.sum(probs * grad_probs, axis=1, keepdims=True)
                grad_scores = (probs * (grad_probs - row_dot)).astype(jnp.bfloat16)
                query_parts.append(
                    jnp.dot(grad_scores, key_rows[:, own], preferred_element_type=jnp.float32)
                )
                key_parts.append(down(grad_scores, queries[:, own]))
            width = heads * HEAD
            gq_ref[first:keys, cols] = (side_by_side(query_parts) * score_scale).astype(
                jnp.bfloat16
            )
            key_sum[0:keys, 0:width] += side_by_side(key_parts)
            value_sum[0:keys, 0:width] += side_by_side(value_parts)
        width = heads * HEAD
        gk_ref[:, cols] = (key_sum[:, 0:width] * score_scale).astype(jnp.bfloat16)
        gv_ref[:, cols] = value_sum[:, 0:width].astype(jnp.bfloat16)

    over_heads(step)


def attend_back(queries, key_rows, value_rows, log_total, grad_mixed, starts):
    count, width = queries.shape
    shape = jax.ShapeDtypeStruct((count, width), jnp.bfloat16)
    return pl.pallas_call(
        attend_back_kernel,
        out_shape=(shape, shape, shape),
        scratch_shapes=[pltpu.VMEM((count, 2 * HEAD), jnp.float32)] * 2,
        compiler_params=pltpu.CompilerParams(vmem_limit_bytes=48 << 20),
        cost_estimate=pl.CostEstimate(
            flops=10 * count * count * width,
            bytes_accessed=14 * count * width,
            transcendentals=HEADS * count * count,
        ),
    )(starts, queries, key_rows, value_rows, log_total, grad_mixed)


def dot_columns(rows, chunks):
    return jnp.concatenate(
        [jnp.dot(rows, chunk, preferred_element_type=jnp.float32) for chunk in chunks], axis=1
    )


def dot_columns_back(rows, chunks):
    width = chunks[0].shape[1]
    return sum(
        jnp.einsum(
            "te,de->td",
            rows[:, i * width : (i + 1) * width],
            chunk,
            preferred_element_type=jnp.float32,
        )
        for i, chunk in enumerate(chunks)
    )


def forward_layer(stream, weights, starts, layout):
    small, qkv_weight, out_weight, up_weight, down_weight = weights
    (
        norm1_gain,
        norm1_shift,
        query_bias,
        value_bias,
        out_bias,
        norm2_gain,
        norm2_shift,
        up_bias,
        down_bias,
    ) = small
    normed = layer_norm(
        stream, norm1_gain.astype(jnp.float32), norm1_shift.astype(jnp.float32)
    ).astype(jnp.bfloat16)
    joined = dot_columns(normed, qkv_weight)
    width = stream.shape[1]
    queries = (joined[:, :width] + query_bias.astype(jnp.float32)).astype(jnp.bfloat16)
    key_rows = joined[:, width : 2 * width].astype(jnp.bfloat16)
    value_rows = (joined[:, 2 * width :] + value_bias.astype(jnp.float32)).astype(jnp.bfloat16)
    projected = (queries, key_rows, value_rows)
    mixed, log_total = attend(queries, key_rows, value_rows, starts)
    after_attn = (
        stream
        + dot_columns(mixed, out_weight)
        + out_bias.astype(jnp.float32)
    )
    normed_two = layer_norm(
        after_attn, norm2_gain.astype(jnp.float32), norm2_shift.astype(jnp.float32)
    ).astype(jnp.bfloat16)
    hidden_pre = dot_columns(normed_two, up_weight) + up_bias.astype(jnp.float32)
    activated, slope = gelu_and_slope(hidden_pre)
    activated, slope = lax.optimization_barrier((activated.astype(jnp.bfloat16), slope))
    result = (
        after_attn
        + jnp.dot(activated, down_weight, preferred_element_type=jnp.float32)
        + down_bias.astype(jnp.float32)
    )
    return (
        result,
        (
            stream,
            normed,
            projected,
            mixed,
            log_total,
            after_attn,
            normed_two,
            slope,
            activated,
        ),
    )


def backward_layer(grad_out, weights, saved, starts, layout, pipe, sum_group):
    small, qkv_weight, out_weight, up_weight, down_weight = weights
    (
        norm1_gain,
        norm1_shift,
        query_bias,
        value_bias,
        out_bias,
        norm2_gain,
        norm2_shift,
        up_bias,
        down_bias,
    ) = small
    stream, normed, projected, mixed, log_total, after_attn, normed_two, slope, activated = (
        saved
    )
    grad_branch = grad_out.astype(jnp.bfloat16)
    sum_group("down", down_group(layout, activated, grad_branch))
    grad_branch = pipe.advance(grad_branch)
    grad_down_bias = jnp.sum(grad_branch.astype(jnp.float32), axis=0)
    grad_act = jnp.einsum("td,fd->tf", grad_branch, down_weight, preferred_element_type=jnp.float32)
    grad_pre = (grad_act * slope).astype(jnp.bfloat16)
    sum_group("up", up_group(layout, normed_two, grad_pre))
    grad_pre = pipe.advance(grad_pre)
    grad_up_bias = jnp.sum(grad_pre.astype(jnp.float32), axis=0)
    grad_normed_two = dot_columns_back(grad_pre, up_weight)
    norm_value, norm_pull = jax.vjp(
        layer_norm, after_attn, norm2_gain.astype(jnp.float32), norm2_shift.astype(jnp.float32)
    )
    grad_after, grad_gain_two, grad_shift_two = norm_pull(grad_normed_two)
    grad_after = grad_out + grad_after
    grad_attn = grad_after.astype(jnp.bfloat16)
    grad_out_bias = jnp.sum(grad_attn.astype(jnp.float32), axis=0)
    grad_mixed = dot_columns_back(grad_attn, out_weight).astype(jnp.bfloat16)
    grad_mixed = pipe.advance(grad_mixed)
    thirds = attend_back(*projected, log_total, grad_mixed, starts)
    sum_group("first", first_group(layout, normed, thirds, mixed, grad_attn))
    thirds = pipe.advance(thirds)
    grad_query_bias = jnp.sum(thirds[0].astype(jnp.float32), axis=0)
    grad_value_bias = jnp.sum(thirds[2].astype(jnp.float32), axis=0)
    if len(qkv_weight) == 3:
        pieces = list(thirds)
    else:
        cols = qkv_weight[0].shape[1]
        whole = jnp.concatenate(thirds, axis=1)
        pieces = [whole[:, i * cols : (i + 1) * cols] for i in range(len(qkv_weight))]
    grad_normed = sum(
        jnp.einsum("te,de->td", piece, chunk, preferred_element_type=jnp.float32)
        for piece, chunk in zip(pieces, qkv_weight)
    )
    first_value, first_pull = jax.vjp(
        layer_norm, stream, norm1_gain.astype(jnp.float32), norm1_shift.astype(jnp.float32)
    )
    grad_stream, grad_gain_one, grad_shift_one = first_pull(grad_normed)
    vectors = (
        grad_gain_one,
        grad_shift_one,
        grad_query_bias,
        grad_value_bias,
        grad_out_bias,
        grad_gain_two,
        grad_shift_two,
        grad_up_bias,
        grad_down_bias,
    )
    return (grad_after + grad_stream, vectors)


class Layout:
    def __init__(self, mesh):
        self.copies = mesh.shape["replica"]
        self.shards = mesh.shape["shard"]
        self.across = self.copies // 4
        self.chips = self.copies // 2
        self.crossed = self.across == 2

    def index(self, a, b, c):
        return (a % self.across) * 4 + (b % 2) * 2 + c

    def pairs(self, way):
        out = []
        for i in range(self.copies):
            a, b, c = i // 4, (i // 2) % 2, i % 2
            turned = self.crossed and c == 1
            if way == "core":
                to = self.index(a, b, 1 - c)
            elif (way == "first") != turned:
                to = self.index(a, b + 1, c)
            else:
                to = self.index(a + 1, b, c)
            out.append((i, to))
        return out

    def move(self, value, way):
        return lax.ppermute(value, "replica", self.pairs(way))

    def place(self):
        r = lax.axis_index("replica")
        return r // 4, (r // 2) % 2, r % 2, lax.axis_index("shard")

    def chip_at(self, core, f, k):
        a, b, _, _ = self.place()
        plain = ((a + k) % self.across) * 2 + (b + f) % 2
        if not self.crossed:
            return plain
        turned = ((a + f) % self.across) * 2 + (b + k) % 2
        return jnp.where(core == 1, turned, plain)

    def slots(self):
        return [(f, k) for k in range(self.across) for f in range(2)]


def place_kernel(by_shard, index_ref, *refs):
    count = len(refs) - 2
    blocks, out_ref, sems = refs[:count], refs[count], refs[count + 1]
    shards = blocks[0].shape[0]
    copies = []
    for p in range(count):
        chip, core = index_ref[0, p], index_ref[1, p]
        for s in range(shards):
            target = out_ref.at[s, chip, core] if by_shard else out_ref.at[chip, s, core]
            copies.append(pltpu.make_async_copy(blocks[p].at[s], target, sems.at[p * shards + s]))
            copies[-1].start()
    for copy in copies:
        copy.wait()


def assemble(layout, blocks, by_shard):
    _, _, core, _ = layout.place()
    chips, shards = layout.chips, layout.shards
    own = [layout.chip_at(core, -f, -k) for f, k in layout.slots()]
    other = [layout.chip_at(1 - core, -f, -k) for f, k in layout.slots()]
    count = 2 * chips
    index = jnp.stack([jnp.stack(own + other), jnp.stack([core] * chips + [1 - core] * chips)])
    _, rows, cols = blocks[0].shape
    outer = (shards, chips) if by_shard else (chips, shards)
    return pl.pallas_call(
        functools.partial(place_kernel, by_shard),
        out_shape=jax.ShapeDtypeStruct(outer + (2, rows, cols), blocks[0].dtype),
        in_specs=[pl.BlockSpec(memory_space=pltpu.SMEM)]
        + [pl.BlockSpec(memory_space=pl.ANY)] * count,
        out_specs=pl.BlockSpec(memory_space=pltpu.VMEM),
        scratch_shapes=[pltpu.SemaphoreType.DMA((count * shards,))],
        compiler_params=pltpu.CompilerParams(vmem_limit_bytes=40 << 20),
        cost_estimate=pl.CostEstimate(
            flops=0, bytes_accessed=4 * count * shards * rows * cols, transcendentals=0
        ),
    )(index.astype(jnp.int32), *blocks)


def gather_group(layout, piece, by_shard, before):
    block = lax.all_gather(piece, "shard", axis=0, tiled=False)
    if before is not None:
        block = lax.optimization_barrier((block, before[0]))[0]
    moved = layout.move(block, "first")
    starts = (block, moved)
    if before is not None:
        starts = lax.optimization_barrier((starts, before[1]))[0]
    held = {(0, 0): starts[0], (1, 0): starts[1]}
    for k in range(1, layout.across):
        for f in range(2):
            held[f, k] = layout.move(held[f, k - 1], "second")
    own = [held[slot] for slot in layout.slots()]
    other = [layout.move(block, "core") for block in own]
    return assemble(layout, own + other, by_shard), (moved, own[2:])


def add_low(left, right):
    return (left.astype(jnp.float32) + right.astype(jnp.float32)).astype(jnp.bfloat16)


def product_kernel(index_ref, rows_ref, cols_ref, *refs):
    total = jnp.dot(rows_ref[0, 0], cols_ref[0], preferred_element_type=jnp.float32)
    if len(refs) == 2:
        total = total + refs[0][0].astype(jnp.float32)
    refs[-1][0] = total.astype(jnp.bfloat16)


def products(rows, cols, index, came=None, skip=0):
    steps = index.shape[1]
    height, width = rows.shape[2], cols.shape[2]
    in_specs = [
        pl.BlockSpec((1, 1) + rows.shape[2:], lambda i, at: (at[0, i], at[1, i], 0, 0)),
        pl.BlockSpec((1,) + cols.shape[1:], lambda i, at: (at[2, i], 0, 0)),
    ]
    operands = [rows, cols]
    if came is not None:
        in_specs.append(pl.BlockSpec((1, height, width), lambda i, at: (i + skip, 0, 0)))
        operands.append(came)
    return pl.pallas_call(
        product_kernel,
        out_shape=jax.ShapeDtypeStruct((steps, height, width), jnp.bfloat16),
        grid_spec=pltpu.PrefetchScalarGridSpec(
            num_scalar_prefetch=1,
            grid=(steps,),
            in_specs=in_specs,
            out_specs=pl.BlockSpec((1, height, width), lambda i, at: (i, 0, 0)),
        ),
        compiler_params=pltpu.CompilerParams(vmem_limit_bytes=40 << 20),
        cost_estimate=pl.CostEstimate(
            flops=2 * steps * height * width * rows.shape[3],
            bytes_accessed=4 * steps * height * width,
            transcendentals=0,
        ),
    )(index, *operands)


def reduce_steps(layout, group, finish):
    rows, cols, blocks_of = group
    _, _, core, _ = layout.place()
    n, last = layout.shards, layout.across - 1
    slots = layout.slots()

    def index(side, wanted):
        places = [blocks_of(layout.chip_at(side, f, k)) for f, k in wanted]
        return jnp.stack(
            [
                jnp.stack([jnp.asarray(i, jnp.int32) for i, _ in places]),
                jnp.stack([side] * len(places)).astype(jnp.int32),
                jnp.stack([jnp.asarray(i, jnp.int32) for _, i in places]),
            ]
        )

    away = products(rows, cols, index(1 - core, slots))
    came = layout.move(away, "core")
    yield [away]
    total = products(rows, cols, index(core, slots[2 * last :]), came, 2 * last)
    moved = layout.move(total, "second")
    kept = products(rows, cols, index(core, slots[: 2 * last]), came, 0)
    yield [total, kept]
    for step in range(1, last):
        total = add_low(moved, kept[2 * (last - step) : 2 * (last - step) + 2])
        moved = layout.move(total, "second")
    sent = add_low(moved[1], kept[1])
    held = add_low(moved[0], kept[0])
    moved = layout.move(sent, "first")
    yield [sent, held]
    total = add_low(moved, held)
    total = total.reshape((n, total.shape[0] // n) + total.shape[1:])
    piece = lax.psum_scatter(total, "shard", scatter_dimension=0, tiled=False)
    yield [total]
    moved = layout.move(piece, "first")
    yield [piece]
    held = [jnp.stack([piece, moved])]
    for _ in range(1, layout.across):
        held.append(layout.move(held[-1], "second"))
    yield [held[0]]
    own = jnp.concatenate(held, axis=0)
    other = layout.move(own, "core")
    yield [own]
    finish(jnp.concatenate([own, other], axis=0))


class Pipe:
    def __init__(self):
        self.running = []

    def begin(self, steps):
        self.running.append(steps)

    def advance(self, value):
        issued, kept = [], []
        for steps in self.running:
            try:
                issued.extend(next(steps))
                kept.append(steps)
            except StopIteration:
                pass
        self.running = kept
        return lax.optimization_barrier((value, issued))[0]

    def drain(self):
        while self.running:
            self.advance(jnp.zeros((), jnp.float32))


def by_core_rows(layout, rows, chips):
    n = layout.shards
    block = rows.T.reshape(n, chips, 2, rows.shape[1] // (2 * n * chips), rows.shape[0])
    return block.transpose(1, 2, 0, 3, 4).reshape(chips, 2, -1, rows.shape[0])


def column_chunks(layout, rows):
    return rows.reshape(rows.shape[0], layout.chips, -1).transpose(1, 0, 2)


def pick(value, i):
    return lax.dynamic_index_in_dim(value, i, axis=0, keepdims=False)


def down_group(layout, activated, grad_branch):
    return by_core_rows(layout, activated, layout.chips), grad_branch[None], lambda chip: (chip, 0)


def up_group(layout, normed_two, grad_pre):
    return by_core_rows(layout, normed_two, 1), column_chunks(layout, grad_pre), lambda chip: (0, chip)


def first_group(layout, normed, thirds, mixed, grad_attn):
    rows = jnp.concatenate([by_core_rows(layout, normed, 1), by_core_rows(layout, mixed, 1)])
    if layout.chips == 4:
        cols = jnp.stack(list(thirds) + [grad_attn])
    else:
        cols = column_chunks(layout, jnp.concatenate(list(thirds) + [grad_attn], axis=1))
    cut = 3 * layout.chips // 4
    return rows, cols, lambda chip: ((chip >= cut).astype(jnp.int32), chip)


def block_order(layout):
    _, _, core, _ = layout.place()
    labels = [layout.chip_at(core, -f, -k) * 2 + core for f, k in layout.slots()]
    labels += [layout.chip_at(1 - core, -f, -k) * 2 + 1 - core for f, k in layout.slots()]
    wanted = jnp.arange(len(labels), dtype=jnp.int32)
    return jnp.argmax(wanted[:, None] == jnp.stack(labels)[None, :], axis=1).astype(jnp.int32)


def sum_vectors(layout, vectors):
    n = layout.shards
    _, _, _, shard = layout.place()
    parts = jnp.concatenate([vector.reshape(n, -1) for vector in vectors], axis=1)
    total = pick(parts, (shard + n - 1) % n)
    for step in range(1, n):
        total = lax.ppermute(total, "shard", [(i, (i + 1) % n) for i in range(n)])
        total = total + pick(parts, (shard + 2 * n - 1 - step) % n)
    bit = 1
    while bit < layout.copies:
        pairs = [(i, i ^ bit) for i in range(layout.copies)]
        total = total + lax.ppermute(total, "replica", pairs)
        bit *= 2
    out, at = [], 0
    for vector in vectors:
        size = vector.shape[0] // n
        out.append(total[at : at + size])
        at += size
    return out


def write_kernel(by_rows, splits, order_ref, blocks_ref, *refs):
    outs = refs[-len(splits) :]
    chips = blocks_ref.shape[0] // 2
    rows, width = blocks_ref.shape[1:]
    if by_rows:
        for i in range(2 * chips):
            outs[0][0, i * rows : (i + 1) * rows, :] = blocks_ref[order_ref[i]].astype(jnp.float32)
        return
    for core in range(2):
        at = 0
        for out, count in zip(outs, splits):
            line = [
                blocks_ref[order_ref[2 * (at + i) + core]].astype(jnp.float32) for i in range(count)
            ]
            out[0, core * rows : (core + 1) * rows, :] = jnp.concatenate(line, axis=1)
            at += count


def write_layer(layout, whole, layer, count, by_rows, splits, held):
    blocks, rows, width = whole.shape
    if by_rows:
        shapes = [(count, blocks * rows, width)]
    else:
        shapes = [(count, 2 * rows, split * width) for split in splits]
    held = [] if held is None else held
    return pl.pallas_call(
        functools.partial(write_kernel, by_rows, splits),
        out_shape=[jax.ShapeDtypeStruct(shape, jnp.float32) for shape in shapes],
        grid=(1,),
        in_specs=[
            pl.BlockSpec(memory_space=pltpu.SMEM),
            pl.BlockSpec(whole.shape, lambda i: (0, 0, 0)),
        ]
        + [pl.BlockSpec(memory_space=pl.ANY)] * len(held),
        out_specs=[
            pl.BlockSpec((1,) + shape[1:], lambda i, layer=layer: (layer, 0, 0)) for shape in shapes
        ],
        input_output_aliases={2 + i: i for i in range(len(held))},
        compiler_params=pltpu.CompilerParams(vmem_limit_bytes=48 << 20),
        cost_estimate=pl.CostEstimate(
            flops=0, bytes_accessed=6 * blocks * rows * width, transcendentals=0
        ),
    )(block_order(layout), whole, *held)


def solution(mesh):
    layout = Layout(mesh)

    def body(
        tokens_in,
        lengths,
        ln1_gain,
        ln1_bias,
        qkv_weight,
        query_bias,
        value_bias,
        out_weight,
        out_bias,
        ln2_gain,
        ln2_bias,
        up_weight,
        up_bias,
        down_weight,
        down_bias,
        cotangent,
    ):
        starts = sequence_starts(lengths, tokens_in.shape[0])
        layer_count = ln1_gain.shape[0]
        chips, shards = layout.chips, layout.shards
        a, b, core, shard = layout.place()
        chip = a * 2 + b

        vectors_in = (
            ln1_gain,
            ln1_bias,
            query_bias,
            value_bias,
            out_bias,
            ln2_gain,
            ln2_bias,
            up_bias,
            down_bias,
        )
        joined = lax.all_gather(jnp.concatenate(vectors_in, axis=1), "shard", axis=0, tiled=False)

        def own_columns(weight):
            rows, cols = weight.shape[0] // 2, weight.shape[1] // chips
            return lax.dynamic_slice(weight, (core * rows, chip * cols), (rows, cols))

        def own_first(one, two):
            cut = 3 * chips // 4
            rows, cols = one.shape[0] // 2, one.shape[1] // cut
            from_one = lax.dynamic_slice(
                one, (core * rows, jnp.minimum(chip, cut - 1) * cols), (rows, cols)
            )
            from_two = lax.dynamic_slice(
                two, (core * rows, jnp.maximum(chip - cut, 0) * cols), (rows, cols)
            )
            return jnp.where(chip < cut, from_one, from_two)

        def own_rows(weight):
            rows = weight.shape[0] // (2 * chips)
            return lax.dynamic_slice_in_dim(weight, (chip * 2 + core) * rows, rows, axis=0)

        weights, before = [], None
        for l in range(layer_count):
            first, before = gather_group(
                layout, own_first(qkv_weight[l], out_weight[l]), False, before
            )
            up, before = gather_group(layout, own_columns(up_weight[l]), False, before)
            down, before = gather_group(layout, own_rows(down_weight[l]), True, before)
            first = first.reshape(chips, -1, first.shape[-1])
            up = up.reshape(chips, -1, up.shape[-1])
            down = down.reshape(-1, down.shape[-1])
            small, at = [], 0
            for vector in vectors_in:
                size = vector.shape[1]
                small.append(joined[:, l, at : at + size].reshape(shards * size))
                at += size
            cut = 3 * chips // 4
            weights.append(
                (
                    small,
                    [first[i] for i in range(cut)],
                    [first[i] for i in range(cut, chips)],
                    [up[i] for i in range(chips)],
                    down,
                )
            )

        stream = tokens_in.astype(jnp.float32)
        saved_all = []
        for l in range(layer_count):
            stream, saved = forward_layer(stream, weights[l], starts, layout)
            saved_all.append(saved)
        block_out = stream.astype(jnp.bfloat16)
        grad_stream = cotangent.astype(jnp.float32)
        shares = [None] * layer_count
        pipe = Pipe()
        held = {"first": None, "up": None, "down": None}

        def sum_group(name, l, group):
            cut = 3 * chips // 4
            splits = (cut, chips - cut) if name == "first" else (chips,)

            def finish(whole):
                held[name] = write_layer(
                    layout, whole, l, layer_count, name == "down", splits, held[name]
                )

            pipe.begin(reduce_steps(layout, group, finish))

        for l in reversed(range(layer_count)):
            grad_stream, vectors = backward_layer(
                grad_stream,
                weights[l],
                saved_all[l],
                starts,
                layout,
                pipe,
                lambda name, group, l=l: sum_group(name, l, group),
            )
            shares[l] = sum_vectors(layout, vectors)
        pipe.drain()

        def stacked(i):
            return jnp.stack([share[i] for share in shares])

        return (
            block_out,
            grad_stream,
            stacked(0),
            stacked(1),
            held["first"][0],
            stacked(2),
            stacked(3),
            held["first"][1],
            stacked(4),
            stacked(5),
            stacked(6),
            held["up"][0],
            stacked(7),
            held["down"][0],
            stacked(8),
        )

    rows = P(("replica", "shard"), None)
    vector = P(None, "shard")
    matrix = P(None, "shard", None)
    params = (
        vector,
        vector,
        matrix,
        vector,
        vector,
        matrix,
        vector,
        vector,
        vector,
        matrix,
        vector,
        matrix,
        vector,
    )
    return jax.shard_map(
        body,
        mesh=mesh,
        in_specs=(rows, rows) + params + (rows,),
        out_specs=(rows, rows) + params,
        check_vma=False,
    )
```

```python
import functools

import jax
import jax.numpy as jnp
from jax import lax
from jax.experimental import pallas as pl
from jax.experimental.pallas import tpu as pltpu
from jax.sharding import PartitionSpec as P

HEADS = 17
HEAD = 64


norm_eps = 1e-05
score_scale = 0.125
masked_fill = -1e30


def layer_norm(values, norm_gain, norm_shift):
    center = values - jnp.mean(values, axis=-1, keepdims=True)
    spread = jnp.mean(center * center, axis=-1, keepdims=True)
    return center * lax.rsqrt(spread + norm_eps) * norm_gain + norm_shift


def gelu_and_slope(values):
    inner = 0.7978845608028654 * (values + 0.044715 * values * values * values)
    bend = jnp.tanh(inner)
    value = 0.5 * values * (1.0 + bend)
    rate = 0.7978845608028654 * (1.0 + 0.134145 * values * values)
    slope = 0.5 * (1.0 + bend) + 0.5 * values * (1.0 - bend * bend) * rate
    return value, slope


def sequence_starts(lengths, count):
    seq_ends = jnp.cumsum(lengths[0])
    positions = jnp.arange(count, dtype=jnp.int32)
    passed = positions[:, None] >= seq_ends[None, :]
    return jnp.max(jnp.where(passed, seq_ends[None, :], 0), axis=1, keepdims=True)


def rows_at_once(count):
    return 256 if count % 256 == 0 else count


def mask_add(starts_ref, first, rows, keys):
    at = lax.broadcasted_iota(jnp.int32, (rows, keys), 0) + first
    key = lax.broadcasted_iota(jnp.int32, (rows, keys), 1)
    allowed = (key <= at) & (key >= starts_ref[first : first + rows, :])
    return jnp.where(allowed, 0.0, masked_fill)


def across(left, right):
    return lax.dot_general(
        left, right, (((1,), (1,)), ((), ())), preferred_element_type=jnp.float32
    )


def down(left, right):
    return lax.dot_general(
        left, right, (((0,), (0,)), ((), ())), preferred_element_type=jnp.float32
    )


def over_heads(step):
    def pair(i, _):
        step(pl.multiple_of(i * 2 * HEAD, 2 * HEAD), 2, i)
        return 0

    lax.fori_loop(0, HEADS // 2, pair, 0)
    if HEADS % 2:
        step((HEADS - 1) * HEAD, 1, HEADS // 2)


def side_by_side(parts):
    return parts[0] if len(parts) == 1 else jnp.concatenate(parts, axis=1)


def attend_kernel(starts_ref, q_ref, k_ref, v_ref, mixed_ref, log_ref):
    count = q_ref.shape[0]
    rows = rows_at_once(count)
    for first in range(0, count, rows):
        keys = first + rows
        mask = mask_add(starts_ref, first, rows, keys)

        def step(at, heads, pair, first=first, keys=keys, mask=mask):
            cols = pl.ds(at, heads * HEAD)
            queries = q_ref[first:keys, cols]
            key_rows = k_ref[0:keys, cols]
            value_rows = v_ref[0:keys, cols]
            mixed = []
            for h in range(heads):
                own = slice(h * HEAD, (h + 1) * HEAD)
                scores = across(queries[:, own], key_rows[:, own]) * score_scale + mask
                row_max = jnp.max(scores, axis=1, keepdims=True)
                exponent = jnp.exp(scores - row_max)
                totals = jnp.sum(exponent, axis=1, keepdims=True)
                probs = (exponent * (1.0 / totals)).astype(jnp.bfloat16)
                mixed.append(
                    jnp.dot(probs, value_rows[:, own], preferred_element_type=jnp.float32)
                )
                log_ref[pair * 2 + h, first:keys, :] = row_max + jnp.log(totals)
            mixed_ref[first:keys, cols] = side_by_side(mixed).astype(jnp.bfloat16)

        over_heads(step)


def attend(queries, key_rows, value_rows, starts):
    count, width = queries.shape
    return pl.pallas_call(
        attend_kernel,
        out_shape=(
            jax.ShapeDtypeStruct((count, width), jnp.bfloat16),
            jax.ShapeDtypeStruct((HEADS, count, 1), jnp.float32),
        ),
        compiler_params=pltpu.CompilerParams(vmem_limit_bytes=48 << 20),
        cost_estimate=pl.CostEstimate(
            flops=4 * count * count * width,
            bytes_accessed=8 * count * width,
            transcendentals=HEADS * count * count,
        ),
    )(starts, queries, key_rows, value_rows)


def attend_back_kernel(
    starts_ref, q_ref, k_ref, v_ref, log_ref, g_ref, gq_ref, gk_ref, gv_ref, key_sum, value_sum
):
    count = q_ref.shape[0]
    rows = rows_at_once(count)
    masks = [mask_add(starts_ref, first, rows, first + rows) for first in range(0, count, rows)]

    def step(at, heads, pair):
        cols = pl.ds(at, heads * HEAD)
        key_sum[...] = jnp.zeros_like(key_sum)
        value_sum[...] = jnp.zeros_like(value_sum)
        for first, mask in zip(range(0, count, rows), masks):
            keys = first + rows
            queries, grads = q_ref[first:keys, cols], g_ref[first:keys, cols]
            key_rows, value_rows = k_ref[0:keys, cols], v_ref[0:keys, cols]
            query_parts, key_parts, value_parts = [], [], []
            for h in range(heads):
                own = slice(h * HEAD, (h + 1) * HEAD)
                scores = across(queries[:, own], key_rows[:, own]) * score_scale + mask
                probs = jnp.exp(scores - log_ref[pair * 2 + h, first:keys, :])
                value_parts.append(down(probs.astype(jnp.bfloat16), grads[:, own]))
                grad_probs = across(grads[:, own], value_rows[:, own])
                row_dot = jnp.sum(probs * grad_probs, axis=1, keepdims=True)
                grad_scores = (probs * (grad_probs - row_dot)).astype(jnp.bfloat16)
                query_parts.append(
                    jnp.dot(grad_scores, key_rows[:, own], preferred_element_type=jnp.float32)
                )
                key_parts.append(down(grad_scores, queries[:, own]))
            width = heads * HEAD
            gq_ref[first:keys, cols] = (side_by_side(query_parts) * score_scale).astype(
                jnp.bfloat16
            )
            key_sum[0:keys, 0:width] += side_by_side(key_parts)
            value_sum[0:keys, 0:width] += side_by_side(value_parts)
        width = heads * HEAD
        gk_ref[:, cols] = (key_sum[:, 0:width] * score_scale).astype(jnp.bfloat16)
        gv_ref[:, cols] = value_sum[:, 0:width].astype(jnp.bfloat16)

    over_heads(step)


def attend_back(queries, key_rows, value_rows, log_total, grad_mixed, starts):
    count, width = queries.shape
    shape = jax.ShapeDtypeStruct((count, width), jnp.bfloat16)
    return pl.pallas_call(
        attend_back_kernel,
        out_shape=(shape, shape, shape),
        scratch_shapes=[pltpu.VMEM((count, 2 * HEAD), jnp.float32)] * 2,
        compiler_params=pltpu.CompilerParams(vmem_limit_bytes=48 << 20),
        cost_estimate=pl.CostEstimate(
            flops=10 * count * count * width,
            bytes_accessed=14 * count * width,
            transcendentals=HEADS * count * count,
        ),
    )(starts, queries, key_rows, value_rows, log_total, grad_mixed)


def dot_columns(rows, chunks):
    return jnp.concatenate(
        [jnp.dot(rows, chunk, preferred_element_type=jnp.float32) for chunk in chunks], axis=1
    )


def dot_columns_back(rows, chunks):
    width = chunks[0].shape[1]
    return sum(
        jnp.einsum(
            "te,de->td",
            rows[:, i * width : (i + 1) * width],
            chunk,
            preferred_element_type=jnp.float32,
        )
        for i, chunk in enumerate(chunks)
    )


def forward_layer(stream, weights, starts, layout):
    small, qkv_weight, out_weight, up_weight, down_weight = weights
    (
        norm1_gain,
        norm1_shift,
        query_bias,
        value_bias,
        out_bias,
        norm2_gain,
        norm2_shift,
        up_bias,
        down_bias,
    ) = small
    normed = layer_norm(
        stream, norm1_gain.astype(jnp.float32), norm1_shift.astype(jnp.float32)
    ).astype(jnp.bfloat16)
    joined = dot_columns(normed, qkv_weight)
    width = stream.shape[1]
    queries = (joined[:, :width] + query_bias.astype(jnp.float32)).astype(jnp.bfloat16)
    key_rows = joined[:, width : 2 * width].astype(jnp.bfloat16)
    value_rows = (joined[:, 2 * width :] + value_bias.astype(jnp.float32)).astype(jnp.bfloat16)
    projected = (queries, key_rows, value_rows)
    mixed, log_total = attend(queries, key_rows, value_rows, starts)
    after_attn = (
        stream
        + dot_columns(mixed, out_weight)
        + out_bias.astype(jnp.float32)
    )
    normed_two = layer_norm(
        after_attn, norm2_gain.astype(jnp.float32), norm2_shift.astype(jnp.float32)
    ).astype(jnp.bfloat16)
    hidden_pre = dot_columns(normed_two, up_weight) + up_bias.astype(jnp.float32)
    activated, slope = gelu_and_slope(hidden_pre)
    activated, slope = lax.optimization_barrier((activated.astype(jnp.bfloat16), slope))
    result = (
        after_attn
        + jnp.dot(activated, down_weight, preferred_element_type=jnp.float32)
        + down_bias.astype(jnp.float32)
    )
    return (
        result,
        (
            stream,
            normed,
            projected,
            mixed,
            log_total,
            after_attn,
            normed_two,
            slope,
            activated,
        ),
    )


def backward_layer(grad_out, weights, saved, starts, layout, pipe, sum_group):
    small, qkv_weight, out_weight, up_weight, down_weight = weights
    (
        norm1_gain,
        norm1_shift,
        query_bias,
        value_bias,
        out_bias,
        norm2_gain,
        norm2_shift,
        up_bias,
        down_bias,
    ) = small
    stream, normed, projected, mixed, log_total, after_attn, normed_two, slope, activated = (
        saved
    )
    grad_branch = grad_out.astype(jnp.bfloat16)
    sum_group("down", down_group(layout, activated, grad_branch))
    grad_branch = pipe.advance(grad_branch)
    grad_down_bias = jnp.sum(grad_branch.astype(jnp.float32), axis=0)
    grad_act = jnp.einsum("td,fd->tf", grad_branch, down_weight, preferred_element_type=jnp.float32)
    grad_pre = (grad_act * slope).astype(jnp.bfloat16)
    sum_group("up", up_group(layout, normed_two, grad_pre))
    grad_pre = pipe.advance(grad_pre)
    grad_up_bias = jnp.sum(grad_pre.astype(jnp.float32), axis=0)
    grad_normed_two = dot_columns_back(grad_pre, up_weight)
    norm_value, norm_pull = jax.vjp(
        layer_norm, after_attn, norm2_gain.astype(jnp.float32), norm2_shift.astype(jnp.float32)
    )
    grad_after, grad_gain_two, grad_shift_two = norm_pull(grad_normed_two)
    grad_after = grad_out + grad_after
    grad_attn = grad_after.astype(jnp.bfloat16)
    grad_out_bias = jnp.sum(grad_attn.astype(jnp.float32), axis=0)
    grad_mixed = dot_columns_back(grad_attn, out_weight).astype(jnp.bfloat16)
    grad_mixed = pipe.advance(grad_mixed)
    thirds = attend_back(*projected, log_total, grad_mixed, starts)
    sum_group("first", first_group(layout, normed, thirds, mixed, grad_attn))
    thirds = pipe.advance(thirds)
    grad_query_bias = jnp.sum(thirds[0].astype(jnp.float32), axis=0)
    grad_value_bias = jnp.sum(thirds[2].astype(jnp.float32), axis=0)
    if len(qkv_weight) == 3:
        pieces = list(thirds)
    else:
        cols = qkv_weight[0].shape[1]
        whole = jnp.concatenate(thirds, axis=1)
        pieces = [whole[:, i * cols : (i + 1) * cols] for i in range(len(qkv_weight))]
    grad_normed = sum(
        jnp.einsum("te,de->td", piece, chunk, preferred_element_type=jnp.float32)
        for piece, chunk in zip(pieces, qkv_weight)
    )
    grad_normed = pipe.advance(grad_normed)
    first_value, first_pull = jax.vjp(
        layer_norm, stream, norm1_gain.astype(jnp.float32), norm1_shift.astype(jnp.float32)
    )
    grad_stream, grad_gain_one, grad_shift_one = first_pull(grad_normed)
    vectors = (
        grad_gain_one,
        grad_shift_one,
        grad_query_bias,
        grad_value_bias,
        grad_out_bias,
        grad_gain_two,
        grad_shift_two,
        grad_up_bias,
        grad_down_bias,
    )
    return (grad_after + grad_stream, vectors)


class Layout:
    def __init__(self, mesh):
        self.copies = mesh.shape["replica"]
        self.shards = mesh.shape["shard"]
        self.across = self.copies // 4
        self.chips = self.copies // 2
        self.crossed = self.across == 2

    def index(self, a, b, c):
        return (a % self.across) * 4 + (b % 2) * 2 + c

    def pairs(self, way):
        out = []
        for i in range(self.copies):
            a, b, c = i // 4, (i // 2) % 2, i % 2
            turned = self.crossed and c == 1
            if way == "core":
                to = self.index(a, b, 1 - c)
            elif (way == "first") != turned:
                to = self.index(a, b + 1, c)
            else:
                to = self.index(a + 1, b, c)
            out.append((i, to))
        return out

    def move(self, value, way):
        return lax.ppermute(value, "replica", self.pairs(way))

    def place(self):
        r = lax.axis_index("replica")
        return r // 4, (r // 2) % 2, r % 2, lax.axis_index("shard")

    def chip_at(self, core, f, k):
        a, b, _, _ = self.place()
        plain = ((a + k) % self.across) * 2 + (b + f) % 2
        if not self.crossed:
            return plain
        turned = ((a + f) % self.across) * 2 + (b + k) % 2
        return jnp.where(core == 1, turned, plain)

    def slots(self):
        return [(f, k) for k in range(self.across) for f in range(2)]


def place_kernel(by_shard, index_ref, *refs):
    count = len(refs) - 2
    blocks, out_ref, sems = refs[:count], refs[count], refs[count + 1]
    shards = blocks[0].shape[0]
    copies = []
    for p in range(count):
        chip, core = index_ref[0, p], index_ref[1, p]
        for s in range(shards):
            target = out_ref.at[s, chip, core] if by_shard else out_ref.at[chip, s, core]
            copies.append(pltpu.make_async_copy(blocks[p].at[s], target, sems.at[p * shards + s]))
            copies[-1].start()
    for copy in copies:
        copy.wait()


def assemble(layout, blocks, by_shard):
    _, _, core, _ = layout.place()
    chips, shards = layout.chips, layout.shards
    own = [layout.chip_at(core, -f, -k) for f, k in layout.slots()]
    other = [layout.chip_at(1 - core, -f, -k) for f, k in layout.slots()]
    count = 2 * chips
    index = jnp.stack([jnp.stack(own + other), jnp.stack([core] * chips + [1 - core] * chips)])
    _, rows, cols = blocks[0].shape
    outer = (shards, chips) if by_shard else (chips, shards)
    return pl.pallas_call(
        functools.partial(place_kernel, by_shard),
        out_shape=jax.ShapeDtypeStruct(outer + (2, rows, cols), blocks[0].dtype),
        in_specs=[pl.BlockSpec(memory_space=pltpu.SMEM)]
        + [pl.BlockSpec(memory_space=pl.ANY)] * count,
        out_specs=pl.BlockSpec(memory_space=pltpu.VMEM),
        scratch_shapes=[pltpu.SemaphoreType.DMA((count * shards,))],
        compiler_params=pltpu.CompilerParams(vmem_limit_bytes=40 << 20),
        cost_estimate=pl.CostEstimate(
            flops=0, bytes_accessed=4 * count * shards * rows * cols, transcendentals=0
        ),
    )(index.astype(jnp.int32), *blocks)


def gather_group(layout, piece, by_shard, before):
    block = lax.all_gather(piece, "shard", axis=0, tiled=False)
    if before is not None:
        block = lax.optimization_barrier((block, before[0]))[0]
    moved = layout.move(block, "first")
    starts = (block, moved)
    if before is not None:
        starts = lax.optimization_barrier((starts, before[1]))[0]
    held = {(0, 0): starts[0], (1, 0): starts[1]}
    for k in range(1, layout.across):
        for f in range(2):
            held[f, k] = layout.move(held[f, k - 1], "second")
    own = [held[slot] for slot in layout.slots()]
    other = [layout.move(block, "core") for block in own]
    return assemble(layout, own + other, by_shard), (moved, own[2:])


def add_low(left, right):
    return (left.astype(jnp.float32) + right.astype(jnp.float32)).astype(jnp.bfloat16)


def product_kernel(index_ref, rows_ref, cols_ref, *refs):
    total = jnp.dot(rows_ref[0, 0], cols_ref[0], preferred_element_type=jnp.float32)
    if len(refs) == 2:
        total = total + refs[0][0].astype(jnp.float32)
    refs[-1][0] = total.astype(jnp.bfloat16)


def products(rows, cols, index, came=None, skip=0):
    steps = index.shape[1]
    height, width = rows.shape[2], cols.shape[2]
    in_specs = [
        pl.BlockSpec((1, 1) + rows.shape[2:], lambda i, at: (at[0, i], at[1, i], 0, 0)),
        pl.BlockSpec((1,) + cols.shape[1:], lambda i, at: (at[2, i], 0, 0)),
    ]
    operands = [rows, cols]
    if came is not None:
        in_specs.append(pl.BlockSpec((1, height, width), lambda i, at: (i + skip, 0, 0)))
        operands.append(came)
    return pl.pallas_call(
        product_kernel,
        out_shape=jax.ShapeDtypeStruct((steps, height, width), jnp.bfloat16),
        grid_spec=pltpu.PrefetchScalarGridSpec(
            num_scalar_prefetch=1,
            grid=(steps,),
            in_specs=in_specs,
            out_specs=pl.BlockSpec((1, height, width), lambda i, at: (i, 0, 0)),
        ),
        compiler_params=pltpu.CompilerParams(vmem_limit_bytes=40 << 20),
        cost_estimate=pl.CostEstimate(
            flops=2 * steps * height * width * rows.shape[3],
            bytes_accessed=4 * steps * height * width,
            transcendentals=0,
        ),
    )(index, *operands)


def reduce_steps(layout, group, finish):
    rows, cols, blocks_of = group
    _, _, core, _ = layout.place()
    n, last = layout.shards, layout.across - 1
    slots = layout.slots()

    def index(side, wanted):
        places = [blocks_of(layout.chip_at(side, f, k)) for f, k in wanted]
        return jnp.stack(
            [
                jnp.stack([jnp.asarray(i, jnp.int32) for i, _ in places]),
                jnp.stack([side] * len(places)).astype(jnp.int32),
                jnp.stack([jnp.asarray(i, jnp.int32) for _, i in places]),
            ]
        )

    away = products(rows, cols, index(1 - core, slots))
    came = layout.move(away, "core")
    yield [away]
    total = products(rows, cols, index(core, slots[2 * last :]), came, 2 * last)
    moved = layout.move(total, "second")
    kept = products(rows, cols, index(core, slots[: 2 * last]), came, 0)
    yield [total, kept]
    for step in range(1, last):
        total = add_low(moved, kept[2 * (last - step) : 2 * (last - step) + 2])
        moved = layout.move(total, "second")
    sent = add_low(moved[1], kept[1])
    held = add_low(moved[0], kept[0])
    moved = layout.move(sent, "first")
    yield [sent, held]
    total = add_low(moved, held)
    total = total.reshape((n, total.shape[0] // n) + total.shape[1:])
    piece = lax.psum_scatter(total, "shard", scatter_dimension=0, tiled=False)
    yield [total]
    moved = layout.move(piece, "first")
    yield [piece]
    held = [jnp.stack([piece, moved])]
    for _ in range(1, layout.across):
        held.append(layout.move(held[-1], "second"))
    yield [held[0]]
    own = jnp.concatenate(held, axis=0)
    other = layout.move(own, "core")
    yield [own]
    finish(jnp.concatenate([own, other], axis=0))


class Pipe:
    def __init__(self):
        self.running = []

    def begin(self, steps):
        self.running.append(steps)

    def advance(self, value):
        issued, kept = [], []
        for steps in self.running:
            try:
                issued.extend(next(steps))
                kept.append(steps)
            except StopIteration:
                pass
        self.running = kept
        return lax.optimization_barrier((value, issued))[0]

    def drain(self):
        while self.running:
            self.advance(jnp.zeros((), jnp.float32))


def by_core_rows(layout, rows, chips):
    n = layout.shards
    block = rows.T.reshape(n, chips, 2, rows.shape[1] // (2 * n * chips), rows.shape[0])
    return block.transpose(1, 2, 0, 3, 4).reshape(chips, 2, -1, rows.shape[0])


def column_chunks(layout, rows):
    return rows.reshape(rows.shape[0], layout.chips, -1).transpose(1, 0, 2)


def pick(value, i):
    return lax.dynamic_index_in_dim(value, i, axis=0, keepdims=False)


def down_group(layout, activated, grad_branch):
    return by_core_rows(layout, activated, layout.chips), grad_branch[None], lambda chip: (chip, 0)


def up_group(layout, normed_two, grad_pre):
    return by_core_rows(layout, normed_two, 1), column_chunks(layout, grad_pre), lambda chip: (0, chip)


def first_group(layout, normed, thirds, mixed, grad_attn):
    rows = jnp.concatenate([by_core_rows(layout, normed, 1), by_core_rows(layout, mixed, 1)])
    if layout.chips == 4:
        cols = jnp.stack(list(thirds) + [grad_attn])
    else:
        cols = column_chunks(layout, jnp.concatenate(list(thirds) + [grad_attn], axis=1))
    cut = 3 * layout.chips // 4
    return rows, cols, lambda chip: ((chip >= cut).astype(jnp.int32), chip)


def block_order(layout):
    _, _, core, _ = layout.place()
    labels = [layout.chip_at(core, -f, -k) * 2 + core for f, k in layout.slots()]
    labels += [layout.chip_at(1 - core, -f, -k) * 2 + 1 - core for f, k in layout.slots()]
    wanted = jnp.arange(len(labels), dtype=jnp.int32)
    return jnp.argmax(wanted[:, None] == jnp.stack(labels)[None, :], axis=1).astype(jnp.int32)


def sum_vectors(layout, vectors):
    n = layout.shards
    _, _, _, shard = layout.place()
    parts = jnp.concatenate([vector.reshape(n, -1) for vector in vectors], axis=1)
    total = pick(parts, (shard + n - 1) % n)
    for step in range(1, n):
        total = lax.ppermute(total, "shard", [(i, (i + 1) % n) for i in range(n)])
        total = total + pick(parts, (shard + 2 * n - 1 - step) % n)
    bit = 1
    while bit < layout.copies:
        pairs = [(i, i ^ bit) for i in range(layout.copies)]
        total = total + lax.ppermute(total, "replica", pairs)
        bit *= 2
    out, at = [], 0
    for vector in vectors:
        size = vector.shape[0] // n
        out.append(total[at : at + size])
        at += size
    return out


def write_kernel(by_rows, splits, order_ref, blocks_ref, *refs):
    outs = refs[-len(splits) :]
    chips = blocks_ref.shape[0] // 2
    rows, width = blocks_ref.shape[1:]
    if by_rows:
        for i in range(2 * chips):
            outs[0][0, i * rows : (i + 1) * rows, :] = blocks_ref[order_ref[i]].astype(jnp.float32)
        return
    for core in range(2):
        at = 0
        for out, count in zip(outs, splits):
            line = [
                blocks_ref[order_ref[2 * (at + i) + core]].astype(jnp.float32) for i in range(count)
            ]
            out[0, core * rows : (core + 1) * rows, :] = jnp.concatenate(line, axis=1)
            at += count


def write_layer(layout, whole, layer, count, by_rows, splits, held):
    blocks, rows, width = whole.shape
    if by_rows:
        shapes = [(count, blocks * rows, width)]
    else:
        shapes = [(count, 2 * rows, split * width) for split in splits]
    held = [] if held is None else held
    return pl.pallas_call(
        functools.partial(write_kernel, by_rows, splits),
        out_shape=[jax.ShapeDtypeStruct(shape, jnp.float32) for shape in shapes],
        grid=(1,),
        in_specs=[
            pl.BlockSpec(memory_space=pltpu.SMEM),
            pl.BlockSpec(whole.shape, lambda i: (0, 0, 0)),
        ]
        + [pl.BlockSpec(memory_space=pl.ANY)] * len(held),
        out_specs=[
            pl.BlockSpec((1,) + shape[1:], lambda i, layer=layer: (layer, 0, 0)) for shape in shapes
        ],
        input_output_aliases={2 + i: i for i in range(len(held))},
        compiler_params=pltpu.CompilerParams(vmem_limit_bytes=48 << 20),
        cost_estimate=pl.CostEstimate(
            flops=0, bytes_accessed=6 * blocks * rows * width, transcendentals=0
        ),
    )(block_order(layout), whole, *held)


def solution(mesh):
    layout = Layout(mesh)

    def body(
        tokens_in,
        lengths,
        ln1_gain,
        ln1_bias,
        qkv_weight,
        query_bias,
        value_bias,
        out_weight,
        out_bias,
        ln2_gain,
        ln2_bias,
        up_weight,
        up_bias,
        down_weight,
        down_bias,
        cotangent,
    ):
        starts = sequence_starts(lengths, tokens_in.shape[0])
        layer_count = ln1_gain.shape[0]
        chips, shards = layout.chips, layout.shards
        a, b, core, shard = layout.place()
        chip = a * 2 + b

        vectors_in = (
            ln1_gain,
            ln1_bias,
            query_bias,
            value_bias,
            out_bias,
            ln2_gain,
            ln2_bias,
            up_bias,
            down_bias,
        )
        joined = lax.all_gather(jnp.concatenate(vectors_in, axis=1), "shard", axis=0, tiled=False)

        def own_columns(weight):
            rows, cols = weight.shape[0] // 2, weight.shape[1] // chips
            return lax.dynamic_slice(weight, (core * rows, chip * cols), (rows, cols))

        def own_first(one, two):
            cut = 3 * chips // 4
            rows, cols = one.shape[0] // 2, one.shape[1] // cut
            from_one = lax.dynamic_slice(
                one, (core * rows, jnp.minimum(chip, cut - 1) * cols), (rows, cols)
            )
            from_two = lax.dynamic_slice(
                two, (core * rows, jnp.maximum(chip - cut, 0) * cols), (rows, cols)
            )
            return jnp.where(chip < cut, from_one, from_two)

        def own_rows(weight):
            rows = weight.shape[0] // (2 * chips)
            return lax.dynamic_slice_in_dim(weight, (chip * 2 + core) * rows, rows, axis=0)

        weights, before = [], None
        for l in range(layer_count):
            first, before = gather_group(
                layout, own_first(qkv_weight[l], out_weight[l]), False, before
            )
            up, before = gather_group(layout, own_columns(up_weight[l]), False, before)
            down, before = gather_group(layout, own_rows(down_weight[l]), True, before)
            first = first.reshape(chips, -1, first.shape[-1])
            up = up.reshape(chips, -1, up.shape[-1])
            down = down.reshape(-1, down.shape[-1])
            small, at = [], 0
            for vector in vectors_in:
                size = vector.shape[1]
                small.append(joined[:, l, at : at + size].reshape(shards * size))
                at += size
            cut = 3 * chips // 4
            weights.append(
                (
                    small,
                    [first[i] for i in range(cut)],
                    [first[i] for i in range(cut, chips)],
                    [up[i] for i in range(chips)],
                    down,
                )
            )

        stream = tokens_in.astype(jnp.float32)
        saved_all = []
        for l in range(layer_count):
            stream, saved = forward_layer(stream, weights[l], starts, layout)
            saved_all.append(saved)
        block_out = stream.astype(jnp.bfloat16)
        grad_stream = cotangent.astype(jnp.float32)
        shares = [None] * layer_count
        pipe = Pipe()
        held = {"first": None, "up": None, "down": None}

        def sum_group(name, l, group):
            cut = 3 * chips // 4
            splits = (cut, chips - cut) if name == "first" else (chips,)

            def finish(whole):
                held[name] = write_layer(
                    layout, whole, l, layer_count, name == "down", splits, held[name]
                )

            pipe.begin(reduce_steps(layout, group, finish))

        for l in reversed(range(layer_count)):
            grad_stream, vectors = backward_layer(
                grad_stream,
                weights[l],
                saved_all[l],
                starts,
                layout,
                pipe,
                lambda name, group, l=l: sum_group(name, l, group),
            )
            shares[l] = vectors
        joint = pipe.advance([vector for vectors in shares for vector in vectors])
        joint = sum_vectors(layout, joint)
        kinds = len(joint) // layer_count
        shares = [joint[l * kinds : (l + 1) * kinds] for l in range(layer_count)]
        pipe.drain()

        def stacked(i):
            return jnp.stack([share[i] for share in shares])

        return (
            block_out,
            grad_stream,
            stacked(0),
            stacked(1),
            held["first"][0],
            stacked(2),
            stacked(3),
            held["first"][1],
            stacked(4),
            stacked(5),
            stacked(6),
            held["up"][0],
            stacked(7),
            held["down"][0],
            stacked(8),
        )

    rows = P(("replica", "shard"), None)
    vector = P(None, "shard")
    matrix = P(None, "shard", None)
    params = (
        vector,
        vector,
        matrix,
        vector,
        vector,
        matrix,
        vector,
        vector,
        vector,
        matrix,
        vector,
        matrix,
        vector,
    )
    return jax.shard_map(
        body,
        mesh=mesh,
        in_specs=(rows, rows) + params + (rows,),
        out_specs=(rows, rows) + params,
        check_vma=False,
    )
```
